256 devices in a mesh: rep: 16 (over x_hi, y, core), fsdp: 16 (over x_lo, z).
Axes of the slice: x: 4 (x_hi: 2, x_lo: 2; x = x_hi * 2 + x_lo), y: 4, z: 8, core: 2. Of those that a mesh axis runs over, the one named last changes fastest.
Arguments:
- features: bfloat16 [16, 8192, 8192], P('rep', 'fsdp'), may hold values from -6 to 6
- targets: bfloat16 [16, 8192, 512], P('rep', 'fsdp'), may hold values from -6 to 6
- value_weight: bfloat16 [16, 8192, 512], P('rep', 'fsdp'), may hold values from -0.0625 to 0.0625
- segment_ids: int32 [16, 8192], P('rep', 'fsdp'), may hold values from -1 to 7, as said below
- traj_counts: int32 [16, 128], P('rep', 'fsdp'), may hold values from 32 to 128
- pseudo_grad: float32 [16, 256, 8192], P('rep', 'fsdp'), may hold values from -6 to 6
- block_exps: int32 [256, 64], P('fsdp'), may hold values from 0 to 3
- outer_params: float32 [256, 8192], P('fsdp'), may hold values from -6 to 6
- outer_moment: float32 [256, 8192], P('fsdp'), may hold values from -3 to 3
Outputs:
- weight_grad: float32 [16, 8192, 512], P('rep', 'fsdp')
- new_params: float32 [256, 8192], P('fsdp')
- new_moment: float32 [256, 8192], P('fsdp')
The draws below stay inside these ranges and needn't reach their ends.
Inputs may be any that keep to these rules, and one draw needn't show every extreme that they name: `segment_ids`: within each aligned block of 512 tokens the ids start at 0 and never decrease over a live prefix of the block, and are -1 after it; every block has 170 or more live tokens.
All inputs are finite; a program needn't handle non-finite values.
Results may differ from the reference program's by a relative error of at most 0.009.
Values may be sent and summed in bfloat16 or wider, within the bound.
A program may use at most 128 MiB of HBM per device.

```python
import math
import jax
import jax.numpy as jnp
from jax import lax

D = 8192
E = 512
SEGS = 8
TOK_DEV = 512
TOKENS = 8192
FRAG = 256
N_REP = 16
N_FSDP = 16


def draw_segment_ids(key, part):
    key = jax.random.fold_in(key, 7)
    key_live, key_start = jax.random.split(key)
    nblocks = N_REP * N_FSDP
    device_pos = jnp.arange(nblocks, dtype=jnp.int32) % N_FSDP
    third = TOK_DEV // 3
    rising = third + device_pos * (TOK_DEV - third) // max(N_FSDP - 1, 1)
    jitter = jax.random.randint(key_live, (nblocks,), 0, TOK_DEV // 16 + 1, dtype=jnp.int32)
    live_len = jnp.maximum(rising - jitter, third)
    starts = jax.random.randint(key_start, (nblocks, SEGS - 1), 1, live_len[:, None], dtype=jnp.int32)
    starts = jnp.sort(starts, axis=1)
    starts = jnp.concatenate([jnp.zeros((nblocks, 1), jnp.int32), starts], axis=1)
    positions = jnp.arange(TOK_DEV, dtype=jnp.int32)
    seg_of = jnp.sum((positions[None, None, :] >= starts[:, :, None]).astype(jnp.int32), axis=1) - 1
    ids = jnp.where(positions[None, :] < live_len[:, None], seg_of, -1)
    return ids.reshape(N_REP, N_FSDP * TOK_DEV).astype(jnp.int32)


def place_ends(array, stream_key, least, largest):
    longest = array.shape.index(max(array.shape))
    spots = []
    for shift in (0, 1):
        where = [jax.random.randint(jax.random.fold_in(stream_key, axis), (), 0, length) for axis, length in enumerate(array.shape)]
        where[longest] = (where[longest] + shift) % array.shape[longest]
        spots.append(tuple(where))
    return array.at[spots[0]].set(least).at[spots[1]].set(largest)


def steps_of(key, extent, shards, smallest, high):
    gain, own = 1.0, jax.random.fold_in(key, 6)
    for axis_at, parts in shards:
        steps = jnp.exp(jax.random.uniform(jax.random.fold_in(own, axis_at), (parts,), jnp.float32, smallest / len(shards), high / len(shards)))
        gain = gain * jnp.repeat(steps, extent[axis_at] // parts).reshape([-1 if axis == axis_at else 1 for axis in range(len(extent))])
    return gain


def bell_draw(rng, dims, width, reach, cuts=(), kind=jnp.bfloat16):
    result = jax.random.normal(rng, dims, jnp.float32) * width
    if len(cuts) > 0:
        result = steps_of(rng, dims, cuts, -0.22, 0.18) * result
    return jnp.clip(result, min=-reach, max=reach).astype(kind)


def setup_inputs(seed: int = 0) -> dict:
    streams_of = jax.random.split(jax.random.key(seed), 10)
    return {
        "features": bell_draw(streams_of[0], (N_REP, TOKENS, D), 1.0, 6.0, ((0, 16), (1, 16))),
        "targets": bell_draw(streams_of[1], (N_REP, TOKENS, E), 1.0, 6.0, ((0, 16), (1, 16))),
        "value_weight": bell_draw(streams_of[2], (N_REP, D, E), D ** -0.5, 0.0625, ((0, 16), (1, 16))),
        "segment_ids": draw_segment_ids(jax.random.fold_in(streams_of[9], 71), 0),
        "traj_counts": place_ends(jax.random.randint(streams_of[4], (N_REP, N_FSDP * SEGS), 32, 129), jax.random.fold_in(streams_of[4], 1), 32, 128).astype(jnp.int32),
        "pseudo_grad": bell_draw(streams_of[5], (N_REP, FRAG, D), 1.0, 6.0, ((0, 16), (1, 16)), jnp.float32),
        "block_exps": place_ends(jax.random.randint(streams_of[6], (FRAG, D // 128), 0, 4), jax.random.fold_in(streams_of[6], 1), 0, 3).astype(jnp.int32),
        "outer_params": bell_draw(streams_of[7], (FRAG, D), 1.0, 6.0, ((0, 16),), jnp.float32),
        "outer_moment": bell_draw(streams_of[8], (FRAG, D), 0.5, 3.0, ((0, 16),), jnp.float32),
    }


BLOCK_WIDTH = 128
SATURATION = 1.0
MOMENTUM = 0.9
OUTER_RATE = 0.7
LOSS_GAIN = 4096.0

def hadamard_table():
    indices = jnp.arange(BLOCK_WIDTH, dtype=jnp.int32)
    masked = jnp.bitwise_and(indices[:, None], indices[None, :])
    parity = jnp.zeros_like(masked)
    for shift in range(7):
        parity = parity + jnp.bitwise_and(jnp.right_shift(masked, shift), 1)
    signs = 1 - 2 * jnp.bitwise_and(parity, 1)
    return signs.astype(jnp.float32) / math.sqrt(BLOCK_WIDTH)

def inner_grad(args):
    feats, targs, weight, seg_ids, counts = args
    live = seg_ids >= 0
    live_total = jnp.sum(live.astype(jnp.float32))
    block_of = jnp.arange(TOKENS, dtype=jnp.int32) // TOK_DEV
    where_idx = (block_of * SEGS + jnp.maximum(seg_ids, 0)).astype(jnp.int32)
    token_count = jnp.take(counts, where_idx).astype(jnp.float32)
    token_count = jnp.where(live, token_count, 1.0)
    predicted = jnp.dot(feats, weight, preferred_element_type=jnp.float32)
    errors = predicted - targs.astype(jnp.float32)
    factor = jnp.where(live, LOSS_GAIN / (token_count * live_total), 0.0)
    scaled = (errors * factor[:, None]).astype(jnp.bfloat16)
    return lax.dot_general(feats, scaled, (((0,), (0,)), ((), ())), preferred_element_type=jnp.float32)

def reference(features, targets, value_weight, segment_ids, traj_counts, pseudo_grad, block_exps, outer_params, outer_moment):
    weight_grad = lax.map(inner_grad, (features, targets, value_weight, segment_ids, traj_counts))
    table = hadamard_table()
    nblocks = D // BLOCK_WIDTH
    scales = jnp.exp2(block_exps.astype(jnp.float32))

    def encode(grad_rows):
        rotated = jnp.einsum('rbk,kj->rbj', grad_rows.reshape(FRAG, nblocks, BLOCK_WIDTH), table, precision=lax.Precision.HIGHEST)
        return jnp.clip(rotated / scales[:, :, None], -SATURATION, SATURATION).astype(jnp.bfloat16)
    encoded = lax.map(encode, pseudo_grad)
    summed = lax.optimization_barrier(jnp.sum(encoded.astype(jnp.float32), axis=0))
    decoded = summed.reshape(FRAG, nblocks, BLOCK_WIDTH) / N_REP * scales[:, :, None]
    delta = jnp.einsum('rbk,kj->rbj', decoded, table, precision=lax.Precision.HIGHEST).reshape(FRAG, D)
    new_moment = MOMENTUM * outer_moment + delta
    new_params = outer_params - OUTER_RATE * (delta + MOMENTUM * new_moment)
    return (weight_grad, new_params, new_moment)
```

```python
import functools
import math

import jax
import jax.numpy as jnp
from jax import lax
from jax.experimental import pallas as pl
from jax.experimental.pallas import tpu as pltpu
from jax.sharding import PartitionSpec as P

MESH = pl.DeviceIdType.MESH
BLOCK_WIDTH = 128
MOMENTUM = 0.9
OUTER_RATE = 0.7
LOSS_GAIN = 4096.0
REPLICAS = 16
NZ = 8
BLK = 512
TOK = 512
WIDTH = 8192
COLS = 256
CHUNKS = 2
X_ROWS = 288
X_PART = (128, 160)
ORDER = (4, 3, -3, 2, -2, 1, -1, 0)
F32 = jnp.float32
BF16 = jnp.bfloat16


def sign_table():
    i = lax.broadcasted_iota(jnp.int32, (BLOCK_WIDTH, BLOCK_WIDTH), 0)
    j = lax.broadcasted_iota(jnp.int32, (BLOCK_WIDTH, BLOCK_WIDTH), 1)
    v = jnp.bitwise_and(i, j)
    for shift in (4, 2, 1):
        v = jnp.bitwise_xor(v, jnp.right_shift(v, shift))
    return (1 - 2 * jnp.bitwise_and(v, 1)).astype(F32).astype(BF16)


def rotate(rows, signs):
    hi = rows.astype(BF16)
    rest = rows - hi.astype(F32)
    mid = rest.astype(BF16)
    low = (rest - mid.astype(F32)).astype(BF16)
    total = jnp.dot(low, signs, preferred_element_type=F32)
    total = total + jnp.dot(mid, signs, preferred_element_type=F32)
    total = total + jnp.dot(hi, signs, preferred_element_type=F32)
    return total * (1.0 / math.sqrt(BLOCK_WIDTH))


def kernel(
    feats_hbm, targs_hbm, weight_hbm, seg_ref, counts_ref, pg_hbm, exps_ref, params_hbm, moment_hbm,
    grad_hbm, newp_hbm, newm_hbm,
    feats, targs, wg, acc, st, xs, xr, z0, zr, fxs, fxr, gt, outw,
    cnt_s, cnt_r, pg, scl, enc, enc_r, par_s, par_r, dlt, params, moment,
    load_sem, store_sem, ss, rs,
):
    r, f = lax.axis_index("rep"), lax.axis_index("fsdp")
    x, z = lax.div(f, NZ), lax.rem(f, NZ)
    xh, g = lax.div(r, 8), lax.rem(r, 8)

    def zz(k):
        return lax.rem(z + (k % NZ), NZ)

    def blk(other, k):
        return ((1 - x) if other else x) * NZ + zz(k)

    zdev = {1: (r, blk(0, 1)), -1: (r, blk(0, -1))}
    xdev = (r, blk(1, 0))
    counter = [0]
    pending = []

    def send(src, dst, target):
        i = counter[0]
        counter[0] += 1
        copy = pltpu.make_async_remote_copy(
            src_ref=src, dst_ref=dst, send_sem=ss.at[i], recv_sem=rs.at[i], device_id=target, device_id_type=MESH
        )
        copy.start()
        pending.append(copy)
        return copy

    loads = {}

    def load(name, src, dst):
        loads[name] = pltpu.make_async_copy(src, dst, load_sem.at[len(loads)])
        loads[name].start()

    for c in range(CHUNKS):
        load(f"w{c}", weight_hbm.at[0, :, pl.ds(c * COLS, COLS)], wg.at[c, f])
    load("pg", pg_hbm.at[0], pg)
    load("feats", feats_hbm.at[0], feats)
    load("targs", targs_hbm.at[0], targs)
    load("params", params_hbm, params)
    load("moment", moment_hbm, moment)

    barrier = pltpu.get_barrier_semaphore()
    for k in range(1, 16):
        pl.semaphore_signal(barrier, inc=1, device_id=(r, lax.rem(f + k, 16)), device_id_type=MESH)
    for k in range(1, 8):
        pl.semaphore_signal(barrier, inc=1, device_id=(xh * 8 + lax.rem(g + k, 8), f), device_id_type=MESH)
    pl.semaphore_signal(barrier, inc=1, device_id=((1 - xh) * 8 + g, f), device_id_type=MESH)

    seg = seg_ref[...]
    live = seg >= 0
    live_here = jnp.sum(live.astype(F32), axis=1, keepdims=True)
    cnt_s[...] = jnp.broadcast_to(live_here, (8, 128))
    tok_count = jnp.zeros((1, TOK), F32)
    counts = counts_ref[...].astype(F32)
    for s in range(8):
        tok_count = tok_count + jnp.where(seg == s, counts[:, s : s + 1], 0.0)
    tok_count = jnp.where(live, tok_count, 1.0)
    pl.semaphore_wait(barrier, 23)

    class Gather:
        def __init__(self, c):
            self.c = c
            self.got = {}
            self.xgot = {}

        def rows(self, j, lo, n):
            return self.ref(j).at[pl.ds(lo, n)]

        def ref(self, j):
            return wg.at[self.c, j]

        def push(self, j, lo, n, target):
            ref = self.rows(j, lo, n)
            return send(ref, ref, target)

        def start(self):
            loads[f"w{self.c}"].wait()
            own = blk(0, 0)
            self.nb = self.push(own, X_ROWS, BLK - X_ROWS, xdev)
            for d in (1, -1):
                self.got[d, 1, "o"] = self.push(own, X_ROWS, BLK - X_ROWS, zdev[d])
            for d in (1, -1):
                self.got[d, 1, "x"] = self.push(own, 0, X_ROWS, zdev[d])
            self.xgot[0] = [self.push(own, 0, X_ROWS, xdev)]

        def cross(self):
            self.nb.wait_recv()
            for d in (1, -1):
                self.got[d, 1, "n"] = self.push(blk(1, 0), X_ROWS, BLK - X_ROWS, zdev[d])

        def step(self, s):
            for name in ("o", "x", "n"):
                for d in (1, -1):
                    self.got[d, s, name].wait_recv()
                    j = blk(name == "n", -d * s)
                    lo, n = (0, X_ROWS) if name == "x" else (X_ROWS, BLK - X_ROWS)
                    hlo, hn = (lo, n // 2) if d == 1 else (lo + n // 2, n // 2)
                    if s < 3:
                        self.got[d, s + 1, name] = self.push(j, lo, n, zdev[d])
                    elif s == 3:
                        self.got[d, s + 1, name] = self.push(j, hlo, hn, zdev[d])
                    if name == "x":
                        flo, fn = (lo, n) if s < 4 else (hlo, hn)
                        key = -d * s if s < 4 else 4
                        self.xgot.setdefault(key, []).append(self.push(j, flo, fn, xdev))

        def product(self, k):
            c = self.c
            total = None
            for kk in ((0,) if k == 0 else (4,) if k == 4 else (k, -k)):
                for copy in self.xgot[kk]:
                    copy.wait_recv()
                for other in (0, 1):
                    j = blk(other, kk)
                    cols = pl.ds(pl.multiple_of(j * BLK, BLK), BLK)
                    part = jnp.dot(feats[:, cols], wg[c, j], preferred_element_type=F32)
                    if k == 0 and total is None:
                        acc[c] = part
                    else:
                        acc[c] += part
                    total = 0

    def scaled(c):
        err = acc[c] - targs[:, c * COLS : (c + 1) * COLS].astype(F32)
        st[c] = (err.T * factor_row()).astype(BF16)

    factor_cache = []

    def factor_row():
        if not factor_cache:
            for copy in counted:
                copy.wait_recv()
            total = live_here
            for k in range(1, 16):
                total = total + cnt_r[k][0:1, 0:1]
            factor_cache.append(jnp.where(live, LOSS_GAIN / (tok_count * total), 0.0))
        return factor_cache[0]

    class Scatter:
        def __init__(self, c):
            self.c = c
            self.nx = X_PART[c]
            self.got = {}
            self.xgot = {}

        def span(self, name):
            return (0, self.nx) if name == "x" else (self.nx, COLS - self.nx)

        def half(self, name, d):
            lo, n = self.span(name)
            return (lo, n // 2) if d == 1 else (lo + n // 2, n // 2)

        def dot(self, other, k, lo, n):
            cols = pl.ds(pl.multiple_of(blk(other, k) * BLK, BLK), BLK)
            return jnp.dot(st[self.c, lo : lo + n], feats[:, cols], preferred_element_type=F32)

        def cross(self, ki):
            c, k = self.c, ORDER[ki]
            lo, n = self.span("x")
            xs[c, ki, 0:n] = self.dot(1, k, lo, n).astype(BF16)
            self.xgot[k] = send(xs.at[c, ki, pl.ds(0, n)], xr.at[c, ki, pl.ds(0, n)], xdev)

        def first(self, names):
            c = self.c
            for name in names:
                lo, n = self.span(name)
                col = 1 if name == "n" else 0
                val = self.dot(col, 4, lo, n)
                if name == "x":
                    self.xgot[4].wait_recv()
                    val = val + xr[c, 0, 0:n].astype(F32)
                z0[c, col, lo : lo + n] = val.astype(BF16)
                for d in (1, -1):
                    hlo, hn = self.half(name, d)
                    self.got[d, 1, name] = send(
                        z0.at[c, col, pl.ds(hlo, hn)], zr.at[c, (1 - d) // 2, 0, col, pl.ds(hlo, hn)], zdev[d]
                    )

        def step(self, s, names=("o", "n", "x")):
            c = self.c
            for name in names:
                lo, n = self.span(name)
                col = 1 if name == "n" else 0
                for d in (1, -1):
                    di = (1 - d) // 2
                    gt[di, lo : lo + n] = self.dot(col, d * (4 - s), lo, n)
                for d in (1, -1):
                    di = (1 - d) // 2
                    k = d * (4 - s)
                    ki = ORDER.index(k)
                    if name == "x":
                        self.xgot[k].wait_recv()
                    self.got[d, s, name].wait_recv()
                    for part in (1, -1):
                        plo, pn = self.half(name, part)
                        val = gt[di, plo : plo + pn]
                        if name == "x":
                            val = val + xr[c, ki, plo : plo + pn].astype(F32)
                        if s > 1 or part == d:
                            val = val + zr[c, di, s - 1, col, plo : plo + pn].astype(F32)
                        zr[c, di, s - 1, col, plo : plo + pn] = val.astype(BF16)
                    self.got[d, s + 1, name] = send(
                        zr.at[c, di, s - 1, col, pl.ds(lo, n)], zr.at[c, di, s, col, pl.ds(lo, n)], zdev[d]
                    )

        def arrived(self, name):
            c = self.c
            lo, n = self.span(name)
            col = 1 if name == "n" else 0
            val = self.dot(col, 0, lo, n)
            if name == "x":
                self.xgot[0].wait_recv()
                val = val + xr[c, ORDER.index(0), 0:n].astype(F32)
            for d in (1, -1):
                self.got[d, 4, name].wait_recv()
                val = val + zr[c, (1 - d) // 2, 3, col, lo : lo + n].astype(F32)
            return val

        def last(self):
            c = self.c
            lo, n = self.span("n")
            fxs[c, 0:n] = self.arrived("n").astype(BF16)
            copy = send(fxs.at[c, pl.ds(0, n)], fxr.at[c, pl.ds(0, n)], xdev)
            gt[0, lo : lo + n] = self.arrived("o")
            gt[0, 0 : self.nx] = self.arrived("x")
            copy.wait_recv()
            gt[0, lo : lo + n] += fxr[c, 0:n].astype(F32)
            outw[c] = gt[0].T
            store(outw.at[c], grad_hbm.at[0, :, pl.ds(c * COLS, COLS)])

    stores = []

    def store(src, dst):
        copy = pltpu.make_async_copy(src, dst, store_sem.at[len(stores)])
        copy.start()
        stores.append(copy)

    nb8 = WIDTH // 8 // BLOCK_WIDTH

    def encode():
        loads["pg"].wait()
        signs = sign_table()
        inv = jnp.right_shift(8, exps_ref[...]).astype(F32) * 0.125
        scale = jnp.left_shift(1, exps_ref[...]).astype(F32)
        for p in range(8):
            base = p * nb8
            rows = jnp.concatenate(
                [pg[:, (base + b) * BLOCK_WIDTH : (base + b + 1) * BLOCK_WIDTH] for b in range(nb8)], axis=0
            )
            turned = rotate(rows, signs)
            for b in range(nb8):
                at = slice(b * BLOCK_WIDTH, (b + 1) * BLOCK_WIDTH)
                val = turned[b * 16 : (b + 1) * 16] * inv[:, base + b : base + b + 1]
                enc[p, :, at] = jnp.clip(val, -1.0, 1.0).astype(BF16)
                scl[p, :, at] = jnp.broadcast_to(scale[:, base + b : base + b + 1], (16, BLOCK_WIDTH))
        out = []
        for k in range(1, 8):
            p = lax.rem(g + k, 8)
            out.append(send(enc.at[p], enc_r.at[k - 1], (xh * 8 + p, f)))
        return out

    def partial_sum(sent):
        total = enc[g].astype(F32)
        for k in range(1, 8):
            sent[k - 1].wait_recv()
            total = total + enc_r[k - 1].astype(F32)
        par_s[...] = total.astype(BF16)
        return send(par_s, par_r, ((1 - xh) * 8 + g, f))

    def decode(sent):
        sent.wait_recv()
        val = (par_s[...].astype(F32) + par_r[...].astype(F32)) * (1.0 / REPLICAS) * scl[g]
        rows = jnp.concatenate([val[:, b * BLOCK_WIDTH : (b + 1) * BLOCK_WIDTH] for b in range(nb8)], axis=0)
        turned = rotate(rows, sign_table()).astype(BF16)
        for b in range(nb8):
            dlt[g, :, b * BLOCK_WIDTH : (b + 1) * BLOCK_WIDTH] = turned[b * 16 : (b + 1) * 16]
        out = []
        for k in range(1, 8):
            p = lax.rem(g + k, 8)
            out.append(send(dlt.at[g], dlt.at[g], (xh * 8 + p, f)))
        return out

    def update(sent):
        for copy in sent:
            copy.wait_recv()
        loads["params"].wait()
        loads["moment"].wait()
        for p in range(8):
            at = slice(p * 1024, (p + 1) * 1024)
            delta = dlt[p].astype(F32)
            new = MOMENTUM * moment[:, at] + delta
            moment[:, at] = new
            params[:, at] = params[:, at] - OUTER_RATE * (delta + MOMENTUM * new)
        store(params, newp_hbm)
        store(moment, newm_hbm)

    g0, g1 = Gather(0), Gather(1)
    s0, s1 = Scatter(0), Scatter(1)
    g0.start()
    counted = [send(cnt_s, cnt_r.at[k], (r, lax.rem(f + k, 16))) for k in range(1, 16)]
    g0.cross()
    sent = encode()
    g0.step(1)
    loads["feats"].wait()
    g0.product(0)
    sent = partial_sum(sent)
    g0.step(2)
    g0.product(1)
    sent = decode(sent)
    g0.step(3)
    g1.start()
    g0.product(2)
    g1.cross()
    g0.step(4)
    update(sent)
    g1.step(1)
    g0.product(3)
    g0.product(4)
    loads["targs"].wait()
    scaled(0)
    g1.product(0)
    g1.step(2)
    g1.product(1)
    s0.cross(0)
    g1.step(3)
    s0.first(("o", "n"))
    g1.product(2)
    s0.cross(1)
    s0.cross(2)
    g1.step(4)
    s0.first(("x",))
    for ki in range(3, 8):
        s0.cross(ki)
    s0.step(1)
    g1.product(3)
    g1.product(4)
    scaled(1)
    s0.step(2)
    for ki in range(0, 8):
        s1.cross(ki)
    s1.first(("o", "n"))
    s0.step(3)
    s1.first(("x",))
    s1.step(1)
    s0.last()
    s1.step(2)
    s1.step(3)
    s1.last()

    for copy in pending:
        copy.wait_send()
    for copy in stores:
        copy.wait()


def on_device(features, targets, value_weight, segment_ids, traj_counts, pseudo_grad, block_exps, outer_params, outer_moment):
    hbm = pl.BlockSpec(memory_space=pl.ANY)
    vmem = pl.BlockSpec(memory_space=pltpu.VMEM)
    xmax = max(X_PART)
    zmax = COLS - min(X_PART)
    n_sem = 256
    out = pl.pallas_call(
        kernel,
        out_shape=(
            jax.ShapeDtypeStruct((1, BLK, 2 * COLS), F32),
            jax.ShapeDtypeStruct((16, WIDTH), F32),
            jax.ShapeDtypeStruct((16, WIDTH), F32),
        ),
        in_specs=[hbm, hbm, hbm, vmem, vmem, hbm, vmem, hbm, hbm],
        out_specs=(hbm, hbm, hbm),
        scratch_shapes=[
            pltpu.VMEM((TOK, WIDTH), BF16),
            pltpu.VMEM((TOK, 2 * COLS), BF16),
            pltpu.VMEM((CHUNKS, 16, BLK, COLS), BF16),
            pltpu.VMEM((CHUNKS, TOK, COLS), F32),
            pltpu.VMEM((CHUNKS, COLS, TOK), BF16),
            pltpu.VMEM((CHUNKS, 8, xmax, BLK), BF16),
            pltpu.VMEM((CHUNKS, 8, xmax, BLK), BF16),
            pltpu.VMEM((CHUNKS, 2, COLS, BLK), BF16),
            pltpu.VMEM((CHUNKS, 2, 4, 2, COLS, BLK), BF16),
            pltpu.VMEM((CHUNKS, zmax, BLK), BF16),
            pltpu.VMEM((CHUNKS, zmax, BLK), BF16),
            pltpu.VMEM((2, COLS, BLK), F32),
            pltpu.VMEM((CHUNKS, BLK, COLS), F32),
            pltpu.VMEM((8, 128), F32),
            pltpu.VMEM((16, 8, 128), F32),
            pltpu.VMEM((16, WIDTH), F32),
            pltpu.VMEM((8, 16, 1024), F32),
            pltpu.VMEM((8, 16, 1024), BF16),
            pltpu.VMEM((7, 16, 1024), BF16),
            pltpu.VMEM((16, 1024), BF16),
            pltpu.VMEM((16, 1024), BF16),
            pltpu.VMEM((8, 16, 1024), BF16),
            pltpu.VMEM((16, WIDTH), F32),
            pltpu.VMEM((16, WIDTH), F32),
            pltpu.SemaphoreType.DMA((8,)),
            pltpu.SemaphoreType.DMA((8,)),
            pltpu.SemaphoreType.DMA((n_sem,)),
            pltpu.SemaphoreType.DMA((n_sem,)),
        ],
        compiler_params=pltpu.CompilerParams(
            collective_id=0, has_side_effects=True, vmem_limit_bytes=56 * 2**20
        ),
    )(features, targets, value_weight, segment_ids, traj_counts, pseudo_grad, block_exps, outer_params, outer_moment)
    return out


def solution(mesh):
    return jax.shard_map(
        on_device,
        mesh=mesh,
        in_specs=(
            P("rep", "fsdp", None),
            P("rep", "fsdp", None),
            P("rep", "fsdp", None),
            P("rep", "fsdp"),
            P("rep", "fsdp"),
            P("rep", "fsdp", None),
            P("fsdp", None),
            P("fsdp", None),
            P("fsdp", None),
        ),
        out_specs=(P("rep", "fsdp", None), P("fsdp", None), P("fsdp", None)),
        check_vma=False,
    )
```

```python
import functools
import math

import jax
import jax.numpy as jnp
from jax import lax
from jax.experimental import pallas as pl
from jax.experimental.pallas import tpu as pltpu
from jax.sharding import PartitionSpec as P

MESH = pl.DeviceIdType.MESH
BLOCK_WIDTH = 128
MOMENTUM = 0.9
OUTER_RATE = 0.7
LOSS_GAIN = 4096.0
REPLICAS = 16
NZ = 8
BLK = 512
TOK = 512
WIDTH = 8192
COLS = 256
CHUNKS = 2
N_SLOTS = 123
EXTRA = 32
X_ROWS = (320, 192)
X_PART = (160, 160)
ORDER = (4, 3, -3, 2, -2, 1, -1, 0)
F32 = jnp.float32
BF16 = jnp.bfloat16
PLAN = (
    ("gs", 0), ("gc", 0), ("gf", 0, 1, "o", 1), ("gf", 0, 1, "o", -1),
    ("enc",), ("gp", 0, 0), ("gf", 0, 1, "x", 1), ("gf", 0, 1, "x", -1),
    ("gf", 0, 1, "n", 1), ("gf", 0, 1, "n", -1), ("par",), ("gf", 0, 2, "o", 1),
    ("gf", 0, 2, "o", -1), ("gf", 0, 2, "x", 1), ("gf", 0, 2, "x", -1), ("gp", 0, 1),
    ("gf", 0, 2, "n", 1), ("gf", 0, 2, "n", -1), ("dec",), ("gf", 0, 3, "o", 1),
    ("gf", 0, 3, "o", -1), ("gf", 0, 3, "x", 1), ("gf", 0, 3, "x", -1), ("upd",),
    ("gp", 0, 2), ("gf", 0, 3, "n", 1), ("gf", 0, 3, "n", -1), ("gs", 1),
    ("gf", 0, 4, "o", 1), ("gf", 0, 4, "o", -1), ("gf", 0, 4, "x", 1), ("gf", 0, 4, "x", -1),
    ("gf", 0, 4, "n", 1), ("gf", 0, 4, "n", -1), ("gp", 0, 3), ("gf", 1, 1, "o", 1),
    ("gf", 1, 1, "o", -1), ("gf", 1, 1, "x", 1), ("gf", 1, 1, "x", -1), ("gc", 1),
    ("gp", 1, 0), ("gf", 1, 2, "o", 1), ("gf", 1, 2, "o", -1), ("gf", 1, 2, "x", 1),
    ("gf", 1, 2, "x", -1), ("gp", 0, 4), ("sc", 0), ("gf", 1, 1, "n", 1),
    ("gf", 1, 1, "n", -1), ("gp", 1, 1), ("rc", 0, 0), ("gf", 1, 3, "o", 1),
    ("gf", 1, 3, "o", -1), ("gf", 1, 3, "x", 1), ("gf", 1, 3, "x", -1), ("rf", 0, "o"),
    ("gf", 1, 2, "n", 1), ("gf", 1, 2, "n", -1), ("gp", 1, 2), ("rc", 0, 1),
    ("gf", 1, 4, "o", 1), ("gf", 1, 4, "o", -1), ("gf", 1, 4, "x", 1), ("gf", 1, 4, "x", -1),
    ("rs", 0, 1, "o", 1), ("rs", 0, 1, "o", -1), ("rf", 0, "n"), ("rc", 0, 2),
    ("gf", 1, 3, "n", 1), ("gf", 1, 3, "n", -1), ("gp", 1, 3), ("rf", 0, "x"),
    ("rs", 0, 2, "o", 1), ("rs", 0, 2, "o", -1), ("rc", 0, 3), ("rs", 0, 1, "n", 1),
    ("rs", 0, 1, "n", -1), ("gf", 1, 4, "n", 1), ("gf", 1, 4, "n", -1), ("gp", 1, 4),
    ("sc", 1), ("rc", 0, 4), ("rs", 0, 1, "x", 1), ("rs", 0, 1, "x", -1),
    ("rs", 0, 3, "o", 1), ("rs", 0, 3, "o", -1), ("rc", 0, 5), ("rs", 0, 2, "n", 1),
    ("rs", 0, 2, "n", -1), ("rc", 0, 6), ("rs", 0, 2, "x", 1), ("rs", 0, 2, "x", -1),
    ("rl", 0, "o"), ("rc", 0, 7), ("rs", 0, 3, "n", 1), ("rs", 0, 3, "n", -1),
    ("rc", 1, 0), ("rf", 1, "o"), ("rs", 0, 3, "x", 1), ("rs", 0, 3, "x", -1),
    ("rc", 1, 1), ("rl", 0, "n"), ("rs", 1, 1, "o", 1), ("rs", 1, 1, "o", -1),
    ("rf", 1, "n"), ("rf", 1, "x"), ("rl", 0, "x"), ("rc", 1, 2),
    ("rs", 1, 2, "o", 1), ("rs", 1, 2, "o", -1), ("rs", 1, 1, "n", 1), ("rs", 1, 1, "n", -1),
    ("fin", 0), ("rc", 1, 3), ("rs", 1, 1, "x", 1), ("rs", 1, 3, "o", 1),
    ("rs", 1, 3, "o", -1), ("rs", 1, 1, "x", -1), ("rc", 1, 4), ("rs", 1, 2, "n", 1),
    ("rs", 1, 2, "n", -1), ("rc", 1, 5), ("rs", 1, 2, "x", 1), ("rl", 1, "o"),
    ("rc", 1, 6), ("rs", 1, 2, "x", -1), ("rs", 1, 3, "n", 1), ("rs", 1, 3, "n", -1),
    ("rc", 1, 7), ("rs", 1, 3, "x", 1), ("rs", 1, 3, "x", -1), ("rl", 1, "n"),
    ("rl", 1, "x"), ("fin", 1),
)


def sign_table():
    i = lax.broadcasted_iota(jnp.int32, (BLOCK_WIDTH, BLOCK_WIDTH), 0)
    j = lax.broadcasted_iota(jnp.int32, (BLOCK_WIDTH, BLOCK_WIDTH), 1)
    v = jnp.bitwise_and(i, j)
    for shift in (4, 2, 1):
        v = jnp.bitwise_xor(v, jnp.right_shift(v, shift))
    return (1 - 2 * jnp.bitwise_and(v, 1)).astype(F32).astype(BF16)


def rotate(rows, signs):
    hi = rows.astype(BF16)
    rest = rows - hi.astype(F32)
    mid = rest.astype(BF16)
    low = (rest - mid.astype(F32)).astype(BF16)
    total = jnp.dot(low, signs, preferred_element_type=F32)
    total = total + jnp.dot(mid, signs, preferred_element_type=F32)
    total = total + jnp.dot(hi, signs, preferred_element_type=F32)
    return total * (1.0 / math.sqrt(BLOCK_WIDTH))


def kernel(
    feats_hbm, targs_hbm, weight_hbm, seg_hbm, counts_hbm, pg_hbm, exps_hbm,
    grad_hbm, delta_hbm,
    feats, targs, wg, acc, st, xs, xr, z0, zr, fxs, fxr, gt, outw,
    pg, scl, enc, landed, par_s, dlt,
    seg_ref, counts_ref, exps_ref, load_sem, store_sem, ss, rs,
):
    r, f = lax.axis_index("rep"), lax.axis_index("fsdp")
    x, z = lax.div(f, NZ), lax.rem(f, NZ)
    xh, g = lax.div(r, 8), lax.rem(r, 8)

    def zz(k):
        return lax.rem(z + (k % NZ), NZ)

    def blk(other, k):
        return ((1 - x) if other else x) * NZ + zz(k)

    zdev = {1: (r, blk(0, 1)), -1: (r, blk(0, -1))}
    xdev = (r, blk(1, 0))
    slots = {}

    def slot(key):
        return rs.at[slots.setdefault(key, len(slots))]

    def send(key, src, dst, target, group):
        pltpu.make_async_remote_copy(
            src_ref=src, dst_ref=dst, send_sem=ss.at[group], recv_sem=slot(key), device_id=target, device_id_type=MESH
        ).start()

    def arrive(key, ref):
        pltpu.make_async_copy(ref, ref, slot(key)).wait()

    def sent(group, ref):
        pltpu.make_async_copy(ref, ref, ss.at[group]).wait()

    loads = {}

    def load(name, src, dst):
        loads[name] = pltpu.make_async_copy(src, dst, load_sem.at[len(loads)])
        loads[name].start()

    for c in range(CHUNKS):
        load(f"w{c}", weight_hbm.at[0, :, pl.ds(c * COLS, COLS)], wg.at[c, f, pl.ds(0, BLK)])
    load("seg", seg_hbm, seg_ref)
    load("counts", counts_hbm, counts_ref)
    load("exps", exps_hbm, exps_ref)
    load("pg", pg_hbm.at[0], pg)
    load("feats", feats_hbm.at[0], feats)
    load("targs", targs_hbm.at[0], targs)

    barrier = pltpu.get_barrier_semaphore()
    for target in (zdev[1], zdev[-1], xdev):
        pl.semaphore_signal(barrier, inc=1, device_id=target, device_id_type=MESH)
    for k in range(1, 8):
        pl.semaphore_signal(barrier, inc=1, device_id=(xh * 8 + lax.rem(g + k, 8), f), device_id_type=MESH)
    pl.semaphore_signal(barrier, inc=1, device_id=((1 - xh) * 8 + g, f), device_id_type=MESH)

    loads["seg"].wait()
    loads["counts"].wait()
    seg = seg_ref[...]
    live = seg >= 0
    live_here = jnp.sum(live.astype(F32), axis=1, keepdims=True)
    tens = jnp.floor(live_here * (1.0 / 16))
    wg[0, f, BLK:, 0:128] = jnp.broadcast_to(tens, (EXTRA, 128)).astype(BF16)
    wg[0, f, BLK:, 128:] = jnp.broadcast_to(live_here - 16 * tens, (EXTRA, COLS - 128)).astype(BF16)
    tok_count = jnp.zeros((1, TOK), F32)
    counts = counts_ref[...].astype(F32)
    for s in range(8):
        tok_count = tok_count + jnp.where(seg == s, counts[:, s : s + 1], 0.0)
    tok_count = jnp.where(live, tok_count, 1.0)
    pl.semaphore_wait(barrier, 11)

    def gather_push(key, c, j, lo, n, target):
        ref = wg.at[c, j, pl.ds(lo, n)]
        send(key, ref, ref, target, c)

    def gather_span(c, name):
        return (0, X_ROWS[c]) if name == "x" else (X_ROWS[c], BLK - X_ROWS[c] + (0 if c else EXTRA))

    def part_of(lo, n, d):
        return (lo, n // 2) if d == 1 else (lo + n // 2, n // 2)

    def gather_start(c):
        loads[f"w{c}"].wait()
        own = blk(0, 0)
        lo, n = gather_span(c, "o")
        if n:
            gather_push(("nb", c), c, own, lo, n, xdev)
        for name in ("o", "x"):
            lo, n = gather_span(c, name)
            if n:
                for d in (1, -1):
                    gather_push(("g", c, d, 1, name), c, own, lo, n, zdev[d])
        if n:
            gather_push(("gx", c, 0), c, own, lo, n, xdev)

    def gather_cross(c):
        lo, n = gather_span(c, "n")
        arrive(("nb", c), wg.at[c, blk(1, 0), pl.ds(lo, n)])
        for d in (1, -1):
            gather_push(("g", c, d, 1, "n"), c, blk(1, 0), lo, n, zdev[d])

    def gather_forward(c, s, name, d):
        j = blk(name == "n", -d * s)
        lo, n = gather_span(c, name)
        half = part_of(lo, n, d)
        arrive(("g", c, d, s, name), wg.at[c, j, pl.ds(*((lo, n) if s < 4 else half))])
        if s < 4:
            at = (lo, n) if s < 3 else half
            gather_push(("g", c, d, s + 1, name), c, j, *at, zdev[d])
        if name == "x":
            at = (lo, n) if s < 4 else half
            gather_push(("gx", c, s), c, j, *at, xdev)

    def product(c, k):
        if k == 0:
            loads_once("feats")
        if X_ROWS[c]:
            lo, n = gather_span(c, "x")
            if k in (0, 4):
                arrive(("gx", c, k), wg.at[c, blk(1, k), pl.ds(lo, n)])
            else:
                arrive(("gx", c, k), wg.at[c, pl.ds(0, 2), pl.ds(lo, n)])
        for kk in (k,) if k in (0, 4) else (k, -k):
            for other in (0, 1):
                j = blk(other, kk)
                cols = pl.ds(pl.multiple_of(j * BLK, BLK), BLK)
                part = jnp.dot(feats[:, cols], wg[c, j, 0:BLK], preferred_element_type=F32)
                if (kk, other) == (0, 0):
                    acc[c] = part
                else:
                    acc[c] += part

    waited = set()

    def loads_once(name):
        if name not in waited:
            waited.add(name)
            loads[name].wait()

    factor_cache = []

    def factor_row():
        if not factor_cache:
            total = jnp.zeros((1, 1), F32)
            for j in range(16):
                digits = wg[0, j, BLK : BLK + 16].astype(F32)
                total = total + (16 * digits[0:1, 0:1] + digits[0:1, 128:129])
            factor_cache.append(jnp.where(live, LOSS_GAIN / (tok_count * total), 0.0))
        return factor_cache[0]

    def scaled(c):
        loads_once("targs")
        err = acc[c] - targs[:, c * COLS : (c + 1) * COLS].astype(F32)
        st[c] = (err.T * factor_row()).astype(BF16)

    def scatter_span(c, name):
        return (0, X_PART[c]) if name == "x" else (X_PART[c], COLS - X_PART[c])

    def share(c, other, k, lo, n):
        cols = pl.ds(pl.multiple_of(blk(other, k) * BLK, BLK), BLK)
        return jnp.dot(st[c, lo : lo + n], feats[:, cols], preferred_element_type=F32)

    def scatter_cross(c, ki):
        k, n = ORDER[ki], X_PART[c]
        xs[c, ki, 0:n] = share(c, 1, k, 0, n).astype(BF16)
        send(("rx", c, k), xs.at[c, ki, pl.ds(0, n)], xr.at[c, ki, pl.ds(0, n)], xdev, 2 + c)

    def crossed(c, k, val):
        ki, n = ORDER.index(k), X_PART[c]
        arrive(("rx", c, k), xr.at[c, ki, pl.ds(0, n)])
        return val + xr[c, ki, 0:n].astype(F32)

    def scatter_first(c, name):
        lo, n = scatter_span(c, name)
        col = 1 if name == "n" else 0
        val = share(c, col, 4, lo, n)
        if name == "x":
            val = crossed(c, 4, val)
        z0[c, col, lo : lo + n] = val.astype(BF16)
        for d in (1, -1):
            hlo, hn = part_of(lo, n, d)
            src, dst = z0.at[c, col, pl.ds(hlo, hn)], zr.at[c, lane(d, 1, col), pl.ds(hlo, hn)]
            send(("r", c, d, 1, name), src, dst, zdev[d], 2 + c)

    def lane(d, s, col):
        return (s - 1) * 4 + col * 2 + (1 - d) // 2

    def scatter_step(c, s, name, d):
        lo, n = scatter_span(c, name)
        col = 1 if name == "n" else 0
        at = lane(d, s, col)
        k = d * (4 - s)
        val = share(c, col, k, lo, n)
        if name == "x":
            val = crossed(c, k, val)
        if s == 1:
            hlo, hn = part_of(lo, n, d)
            olo, on = part_of(lo, n, -d)
            arrive(("r", c, d, s, name), zr.at[c, at, pl.ds(hlo, hn)])
            zr[c, at, olo : olo + on] = val[olo - lo : olo - lo + on].astype(BF16)
            got = zr[c, at, hlo : hlo + hn].astype(F32)
            zr[c, at, hlo : hlo + hn] = (val[hlo - lo : hlo - lo + hn] + got).astype(BF16)
        else:
            arrive(("r", c, d, s, name), zr.at[c, at, pl.ds(lo, n)])
            zr[c, at, lo : lo + n] = (val + zr[c, at, lo : lo + n].astype(F32)).astype(BF16)
        key = ("r", c, d, s + 1, name) if s < 3 else ("r", c, 4, name)
        send(key, zr.at[c, at, pl.ds(lo, n)], zr.at[c, lane(d, s + 1, col), pl.ds(lo, n)], zdev[d], 2 + c)

    def scatter_last(c, name):
        lo, n = scatter_span(c, name)
        col = 1 if name == "n" else 0
        val = share(c, col, 0, lo, n)
        if name == "x":
            val = crossed(c, 0, val)
        arrive(("r", c, 4, name), zr.at[c, pl.ds(lane(1, 4, col), 2), pl.ds(lo, n)])
        for d in (1, -1):
            val = val + zr[c, lane(d, 4, col), lo : lo + n].astype(F32)
        if name == "n":
            fxs[c, 0:n] = val.astype(BF16)
            send(("fin", c), fxs.at[c, pl.ds(0, n)], fxr.at[c, pl.ds(0, n)], xdev, 2 + c)
        else:
            gt[c, lo : lo + n] = val

    def finish(c):
        lo, n = scatter_span(c, "n")
        if n:
            arrive(("fin", c), fxr.at[c, pl.ds(0, n)])
            gt[c, lo : lo + n] += fxr[c, 0:n].astype(F32)
        store(gt.at[c], grad_hbm.at[c])

    stores = []

    def store(src, dst):
        copy = pltpu.make_async_copy(src, dst, store_sem.at[len(stores)])
        copy.start()
        stores.append(copy)

    nb8 = WIDTH // 8 // BLOCK_WIDTH

    def encode():
        loads["exps"].wait()
        loads["pg"].wait()
        signs = sign_table()
        inv = jnp.right_shift(8, exps_ref[...]).astype(F32) * 0.125
        scale = jnp.left_shift(1, exps_ref[...]).astype(F32)
        for p in range(8):
            base = p * nb8
            rows = jnp.concatenate(
                [pg[:, (base + b) * BLOCK_WIDTH : (base + b + 1) * BLOCK_WIDTH] for b in range(nb8)], axis=0
            )
            turned = rotate(rows, signs)
            for b in range(nb8):
                at = slice(b * BLOCK_WIDTH, (b + 1) * BLOCK_WIDTH)
                val = turned[b * 16 : (b + 1) * 16] * inv[:, base + b : base + b + 1]
                enc[p, :, at] = jnp.clip(val, -1.0, 1.0).astype(BF16)
                scl[p, :, at] = jnp.broadcast_to(scale[:, base + b : base + b + 1], (16, BLOCK_WIDTH))
        for k in range(1, 8):
            p = lax.rem(g + k, 8)
            send("enc", enc.at[p], landed.at[k - 1], (xh * 8 + p, f), 4)

    def partial_sum():
        arrive("enc", landed.at[pl.ds(0, 7)])
        total = enc[g].astype(F32)
        for k in range(1, 8):
            total = total + landed[k - 1].astype(F32)
        par_s[...] = total.astype(BF16)
        send("par", par_s, landed.at[7], ((1 - xh) * 8 + g, f), 4)

    def decode():
        arrive("par", landed.at[7])
        val = (par_s[...].astype(F32) + landed[7].astype(F32)) * (1.0 / REPLICAS) * scl[g]
        rows = jnp.concatenate([val[:, b * BLOCK_WIDTH : (b + 1) * BLOCK_WIDTH] for b in range(nb8)], axis=0)
        turned = rotate(rows, sign_table()).astype(BF16)
        mine = pl.ds(pl.multiple_of(g * 1024, 1024), 1024)
        dlt[:, mine] = jnp.concatenate([turned[b * 16 : (b + 1) * 16] for b in range(nb8)], axis=1)
        for k in range(1, 8):
            send("dlt", dlt.at[:, mine], dlt.at[:, mine], (xh * 8 + lax.rem(g + k, 8), f), 4)

    def update():
        arrive("dlt", landed.at[pl.ds(0, 7)])
        store(dlt, delta_hbm)

    steps = {
        "gs": gather_start,
        "gc": gather_cross,
        "gf": gather_forward,
        "gp": product,
        "sc": scaled,
        "rc": scatter_cross,
        "rf": scatter_first,
        "rs": scatter_step,
        "rl": scatter_last,
        "fin": finish,
        "enc": encode,
        "par": partial_sum,
        "dec": decode,
        "upd": update,
    }
    for step in PLAN:
        steps[step[0]](*step[1:])
    assert len(slots) == N_SLOTS, len(slots)

    for c in range(CHUNKS):
        sent(c, wg.at[c, pl.ds(0, 15), pl.ds(0, BLK if c else BLK + EXTRA)])
        sent(2 + c, zr.at[c, pl.ds(0, 15)])
    sent(4, landed)
    for copy in stores:
        copy.wait()


def finish_kernel(gt_hbm, delta_hbm, params_hbm, moment_hbm, grad_hbm, newp_hbm, newm_hbm, gt, dlt, params, moment, out, newp, newm, load_sem, store_sem):
    loads = [
        pltpu.make_async_copy(gt_hbm.at[c], gt.at[c], load_sem.at[c]) for c in range(CHUNKS)
    ] + [
        pltpu.make_async_copy(delta_hbm, dlt, load_sem.at[CHUNKS]),
        pltpu.make_async_copy(params_hbm, params, load_sem.at[CHUNKS + 1]),
        pltpu.make_async_copy(moment_hbm, moment, load_sem.at[CHUNKS + 2]),
    ]
    for copy in loads:
        copy.start()
    stores = []

    def store(src, dst):
        copy = pltpu.make_async_copy(src, dst, store_sem.at[len(stores)])
        copy.start()
        stores.append(copy)

    for c in range(CHUNKS):
        loads[c].wait()
        out[:, c * COLS : (c + 1) * COLS] = gt[c].T
    store(out, grad_hbm.at[0])
    for copy in loads[CHUNKS:]:
        copy.wait()
    delta = dlt[...].astype(F32)
    new = MOMENTUM * moment[...] + delta
    newm[...] = new
    store(newm, newm_hbm)
    newp[...] = params[...] - OUTER_RATE * (delta + MOMENTUM * new)
    store(newp, newp_hbm)
    for copy in stores:
        copy.wait()


def on_device(features, targets, value_weight, segment_ids, traj_counts, pseudo_grad, block_exps, outer_params, outer_moment):
    hbm = pl.BlockSpec(memory_space=pl.ANY)
    xmax = max(X_PART)
    zmax = COLS - min(X_PART)
    out = pl.pallas_call(
        kernel,
        out_shape=(
            jax.ShapeDtypeStruct((CHUNKS, COLS, BLK), F32),
            jax.ShapeDtypeStruct((16, WIDTH), BF16),
        ),
        in_specs=[hbm] * 7,
        out_specs=(hbm, hbm),
        scratch_shapes=[
            pltpu.VMEM((TOK, WIDTH), BF16),
            pltpu.VMEM((TOK, 2 * COLS), BF16),
            pltpu.VMEM((CHUNKS, 16, BLK + EXTRA, COLS), BF16),
            pltpu.VMEM((CHUNKS, TOK, COLS), F32),
            pltpu.VMEM((CHUNKS, COLS, TOK), BF16),
            pltpu.VMEM((CHUNKS, 8, xmax, BLK), BF16),
            pltpu.VMEM((CHUNKS, 8, xmax, BLK), BF16),
            pltpu.VMEM((CHUNKS, 2, COLS, BLK), BF16),
            pltpu.VMEM((CHUNKS, 16, COLS, BLK), BF16),
            pltpu.VMEM((CHUNKS, zmax, BLK), BF16),
            pltpu.VMEM((CHUNKS, zmax, BLK), BF16),
            pltpu.VMEM((CHUNKS, COLS, BLK), F32),
            pltpu.VMEM((CHUNKS, BLK, COLS), F32),
            pltpu.VMEM((16, WIDTH), F32),
            pltpu.VMEM((8, 16, 1024), F32),
            pltpu.VMEM((8, 16, 1024), BF16),
            pltpu.VMEM((15, 16, 1024), BF16),
            pltpu.VMEM((16, 1024), BF16),
            pltpu.VMEM((16, WIDTH), BF16),
            pltpu.VMEM((1, TOK), jnp.int32),
            pltpu.VMEM((1, 8), jnp.int32),
            pltpu.VMEM((16, WIDTH // BLOCK_WIDTH), jnp.int32),
            pltpu.SemaphoreType.DMA((CHUNKS + 6,)),
            pltpu.SemaphoreType.DMA((3,)),
            pltpu.SemaphoreType.DMA((5,)),
            pltpu.SemaphoreType.DMA((N_SLOTS,)),
        ],
        compiler_params=pltpu.CompilerParams(
            collective_id=0, has_side_effects=True, vmem_limit_bytes=56 * 2**20
        ),
    )(features, targets, value_weight, segment_ids, traj_counts, pseudo_grad, block_exps)
    wide = pltpu.VMEM((16, WIDTH), F32)
    return pl.pallas_call(
        finish_kernel,
        out_shape=(
            jax.ShapeDtypeStruct((1, BLK, CHUNKS * COLS), F32),
            jax.ShapeDtypeStruct((16, WIDTH), F32),
            jax.ShapeDtypeStruct((16, WIDTH), F32),
        ),
        in_specs=[hbm] * 4,
        out_specs=(hbm,) * 3,
        scratch_shapes=[
            pltpu.VMEM((CHUNKS, COLS, BLK), F32),
            pltpu.VMEM((16, WIDTH), BF16),
            wide,
            wide,
            pltpu.VMEM((BLK, CHUNKS * COLS), F32),
            wide,
            wide,
            pltpu.SemaphoreType.DMA((CHUNKS + 3,)),
            pltpu.SemaphoreType.DMA((3,)),
        ],
        compiler_params=pltpu.CompilerParams(vmem_limit_bytes=60 * 2**20),
    )(*out, outer_params, outer_moment)


def solution(mesh):
    return jax.shard_map(
        on_device,
        mesh=mesh,
        in_specs=(
            P("rep", "fsdp", None),
            P("rep", "fsdp", None),
            P("rep", "fsdp", None),
            P("rep", "fsdp"),
            P("rep", "fsdp"),
            P("rep", "fsdp", None),
            P("fsdp", None),
            P("fsdp", None),
            P("fsdp", None),
        ),
        out_specs=(P("rep", "fsdp", None), P("fsdp", None), P("fsdp", None)),
        check_vma=False,
    )
```

```python
import functools
import math

import jax
import jax.numpy as jnp
from jax import lax
from jax.experimental import pallas as pl
from jax.experimental.pallas import tpu as pltpu
from jax.sharding import PartitionSpec as P

MESH = pl.DeviceIdType.MESH
BLOCK_WIDTH = 128
MOMENTUM = 0.9
OUTER_RATE = 0.7
LOSS_GAIN = 4096.0
REPLICAS = 16
NZ = 8
BLK = 512
TOK = 512
WIDTH = 8192
COLS = 256
HALF = 256
CHUNKS = 2
N_SLOTS = 124
EXTRA = 32
X_ROWS = (HALF, HALF)
X_PART = (64, 256)
ORDER = (4, 3, -3, 2, -2, 1, -1, 0)
COLUMN = {"o": 0, "x": 0, "n": 1, "b": 2}
F32 = jnp.float32
BF16 = jnp.bfloat16
PLAN = (
    ("gs", 0), ("fx", 0), ("gc", 0), ("gp", 0, 0),
    ("gf", 0, 1, "o", 1), ("gf", 0, 1, "o", -1), ("enc",), ("fx", 1),
    ("gf", 0, 1, "x", 1), ("gf", 0, 1, "x", -1), ("gf", 0, 1, "n", 1), ("gf", 0, 1, "n", -1),
    ("gp", 0, 1), ("fx", 2), ("par",), ("gf", 0, 2, "o", 1),
    ("gf", 0, 2, "o", -1), ("gf", 0, 2, "x", 1), ("gf", 0, 2, "x", -1), ("fx", 3),
    ("dec",), ("gf", 0, 2, "n", 1), ("gf", 0, 2, "n", -1), ("gp", 0, 2),
    ("gf", 0, 3, "o", 1), ("gf", 0, 3, "o", -1), ("fx", 4), ("upd",),
    ("gf", 0, 3, "x", 1), ("gf", 0, 3, "x", -1), ("fx", 5), ("gf", 0, 3, "n", 1),
    ("gf", 0, 3, "n", -1), ("gp", 0, 3), ("gs", 1), ("gf", 0, 4, "o", 1),
    ("gf", 0, 4, "o", -1), ("gf", 0, 4, "x", 1), ("gf", 0, 4, "x", -1), ("gf", 0, 4, "n", 1),
    ("gf", 0, 4, "n", -1), ("gp", 0, 4), ("gf", 1, 1, "o", 1), ("gf", 1, 1, "o", -1),
    ("fx", 6), ("gf", 1, 1, "x", 1), ("gf", 1, 1, "x", -1), ("gf", 1, 2, "o", 1),
    ("gf", 1, 2, "o", -1), ("gc", 1), ("gp", 1, 0), ("fx", 7),
    ("gf", 1, 2, "x", 1), ("gf", 1, 2, "x", -1), ("gf", 1, 3, "o", 1), ("gf", 1, 3, "o", -1),
    ("gf", 1, 1, "n", 1), ("gf", 1, 1, "n", -1), ("gp", 1, 1), ("gq", 0, 0),
    ("gq", 0, 1), ("gf", 1, 3, "x", 1), ("gf", 1, 3, "x", -1), ("gq", 0, 2),
    ("gq", 0, 3), ("gq", 0, 4), ("gq", 1, 0), ("gq", 1, 1),
    ("gf", 1, 4, "o", 1), ("gf", 1, 4, "o", -1), ("gf", 1, 2, "n", 1), ("gf", 1, 2, "n", -1),
    ("gp", 1, 2), ("gq", 1, 2), ("gf", 1, 4, "x", 1), ("gf", 1, 4, "x", -1),
    ("sc", 0), ("ss", 0), ("rf", 0, "o"), ("rf", 0, "n"),
    ("gf", 1, 3, "n", 1), ("gf", 1, 3, "n", -1), ("gp", 1, 3), ("gq", 1, 3),
    ("rc", 0, 0), ("rc", 0, 1), ("rs", 0, 1, "o", 1), ("rs", 0, 1, "o", -1),
    ("rc", 0, 2), ("rs", 0, 1, "n", 1), ("rs", 0, 1, "n", -1), ("rc", 0, 3),
    ("rc", 0, 4), ("gf", 1, 4, "n", 1), ("rc", 0, 5), ("gf", 1, 4, "n", -1),
    ("gp", 1, 4), ("gq", 1, 4), ("rf", 0, "b"), ("rs", 0, 2, "o", 1),
    ("rs", 0, 2, "o", -1), ("rf", 0, "x"), ("rs", 0, 2, "n", 1), ("rs", 0, 2, "n", -1),
    ("rs", 0, 1, "b", 1), ("rs", 0, 1, "b", -1), ("rc", 0, 6), ("rc", 0, 7),
    ("rs", 0, 3, "o", 1), ("rs", 0, 3, "o", -1), ("rs", 0, 1, "x", 1), ("rs", 0, 1, "x", -1),
    ("rs", 0, 3, "n", 1), ("rs", 0, 3, "n", -1), ("sc", 1), ("ss", 1),
    ("rs", 0, 2, "b", 1), ("rs", 0, 2, "b", -1), ("rc", 1, 0), ("rl", 0, "o"),
    ("rs", 0, 2, "x", 1), ("rs", 0, 2, "x", -1), ("rc", 1, 1), ("rl", 0, "n"),
    ("rf", 1, "b"), ("rs", 0, 3, "b", 1), ("rs", 0, 3, "b", -1), ("rc", 1, 2),
    ("rs", 0, 3, "x", 1), ("rs", 0, 3, "x", -1), ("rf", 1, "x"), ("rs", 1, 1, "b", 1),
    ("rs", 1, 1, "b", -1), ("rc", 1, 3), ("rl", 0, "b"), ("rc", 1, 4),
    ("rl", 0, "x"), ("fin", 0), ("rs", 1, 1, "x", 1), ("rs", 1, 1, "x", -1),
    ("rc", 1, 5), ("rs", 1, 2, "b", 1), ("rs", 1, 2, "b", -1), ("rc", 1, 6),
    ("rs", 1, 2, "x", 1), ("rs", 1, 2, "x", -1), ("rc", 1, 7), ("rs", 1, 3, "b", 1),
    ("rs", 1, 3, "b", -1), ("rs", 1, 3, "x", 1), ("rs", 1, 3, "x", -1), ("rl", 1, "b"),
    ("rl", 1, "x"), ("fin", 1),
)


def sign_table():
    i = lax.broadcasted_iota(jnp.int32, (BLOCK_WIDTH, BLOCK_WIDTH), 0)
    j = lax.broadcasted_iota(jnp.int32, (BLOCK_WIDTH, BLOCK_WIDTH), 1)
    v = jnp.bitwise_and(i, j)
    for shift in (4, 2, 1):
        v = jnp.bitwise_xor(v, jnp.right_shift(v, shift))
    return (1 - 2 * jnp.bitwise_and(v, 1)).astype(F32).astype(BF16)


def rotate(rows, signs):
    hi = rows.astype(BF16)
    rest = rows - hi.astype(F32)
    mid = rest.astype(BF16)
    low = (rest - mid.astype(F32)).astype(BF16)
    total = jnp.dot(low, signs, preferred_element_type=F32)
    total = total + jnp.dot(mid, signs, preferred_element_type=F32)
    total = total + jnp.dot(hi, signs, preferred_element_type=F32)
    return total * (1.0 / math.sqrt(BLOCK_WIDTH))


def kernel(
    feats_hbm, targs_hbm, weight_hbm, seg_hbm, counts_hbm, pg_hbm, exps_hbm,
    grad_hbm, delta_hbm,
    feats, targs, wg, acc, st, fnb, accn, ps, pr, stn, xs, xr, z0, zr, fxs, fxr, gt, outw,
    pg, scl, enc, landed, par_s, dlt,
    seg_ref, counts_ref, exps_ref, load_sem, store_sem, ss, rs,
):
    r, f = lax.axis_index("rep"), lax.axis_index("fsdp")
    x, z = lax.div(f, NZ), lax.rem(f, NZ)
    xh, g = lax.div(r, 8), lax.rem(r, 8)

    def zz(k):
        return lax.rem(z + (k % NZ), NZ)

    def blk(other, k):
        return ((1 - x) if other else x) * NZ + zz(k)

    zdev = {1: (r, blk(0, 1)), -1: (r, blk(0, -1))}
    xdev = (r, blk(1, 0))
    slots = {}

    def slot(key):
        return rs.at[slots.setdefault(key, len(slots))]

    def send(key, src, dst, target, group):
        pltpu.make_async_remote_copy(
            src_ref=src, dst_ref=dst, send_sem=ss.at[group], recv_sem=slot(key), device_id=target, device_id_type=MESH
        ).start()

    def arrive(key, ref):
        pltpu.make_async_copy(ref, ref, slot(key)).wait()

    def sent(group, ref):
        pltpu.make_async_copy(ref, ref, ss.at[group]).wait()

    loads = {}

    def load(name, src, dst):
        loads[name] = pltpu.make_async_copy(src, dst, load_sem.at[len(loads)])
        loads[name].start()

    for c in range(CHUNKS):
        load(f"w{c}", weight_hbm.at[0, :, pl.ds(c * COLS, COLS)], wg.at[c, f, pl.ds(0, BLK)])
    load("seg", seg_hbm, seg_ref)
    load("counts", counts_hbm, counts_ref)
    load("exps", exps_hbm, exps_ref)
    load("pg", pg_hbm.at[0], pg)
    load("feats", feats_hbm.at[0], feats)
    load("targs", targs_hbm.at[0], targs)

    barrier = pltpu.get_barrier_semaphore()
    for target in (zdev[1], zdev[-1], xdev):
        pl.semaphore_signal(barrier, inc=1, device_id=target, device_id_type=MESH)
    for k in range(1, 8):
        pl.semaphore_signal(barrier, inc=1, device_id=(xh * 8 + lax.rem(g + k, 8), f), device_id_type=MESH)
    pl.semaphore_signal(barrier, inc=1, device_id=((1 - xh) * 8 + g, f), device_id_type=MESH)

    loads["seg"].wait()
    loads["counts"].wait()
    seg = seg_ref[...]
    live = seg >= 0
    live_here = jnp.sum(live.astype(F32), axis=1, keepdims=True)
    tens = jnp.floor(live_here * (1.0 / 16))
    wg[0, f, BLK:, 0:128] = jnp.broadcast_to(tens, (EXTRA, 128)).astype(BF16)
    wg[0, f, BLK:, 128:] = jnp.broadcast_to(live_here - 16 * tens, (EXTRA, COLS - 128)).astype(BF16)
    tok_count = jnp.zeros((1, TOK), F32)
    counts = counts_ref[...].astype(F32)
    for s in range(8):
        tok_count = tok_count + jnp.where(seg == s, counts[:, s : s + 1], 0.0)
    tok_count = jnp.where(live, tok_count, 1.0)
    pl.semaphore_wait(barrier, 11)

    def gather_push(key, c, j, lo, n, target):
        ref = wg.at[c, j, pl.ds(lo, n)]
        send(key, ref, ref, target, 2 + c if lo < HALF else c)

    def gather_span(c, name):
        return (0, X_ROWS[c]) if name == "x" else (X_ROWS[c], BLK - X_ROWS[c] + (0 if c else EXTRA))

    def part_of(lo, n, d):
        return (lo, n // 2) if d == 1 else (lo + n // 2, n // 2)

    def gather_start(c):
        loads[f"w{c}"].wait()
        own = blk(0, 0)
        lo, n = gather_span(c, "o")
        if n:
            gather_push(("nb", c), c, own, lo, n, xdev)
        for name in ("o", "x"):
            lo, n = gather_span(c, name)
            if n:
                for d in (1, -1):
                    gather_push(("g", c, d, 1, name), c, own, lo, n, zdev[d])

    def gather_cross(c):
        lo, n = gather_span(c, "n")
        arrive(("nb", c), wg.at[c, blk(1, 0), pl.ds(lo, n)])
        for d in (1, -1):
            gather_push(("g", c, d, 1, "n"), c, blk(1, 0), lo, n, zdev[d])

    def gather_forward(c, s, name, d):
        j = blk(name == "n", -d * s)
        lo, n = gather_span(c, name)
        half = part_of(lo, n, d)
        arrive(("g", c, d, s, name), wg.at[c, j, pl.ds(*((lo, n) if s < 4 else half))])
        if s < 4:
            at = (lo, n) if s < 3 else half
            gather_push(("g", c, d, s + 1, name), c, j, *at, zdev[d])

    def product(c, k):
        if k == 0:
            loads_once("feats")
        for kk in (k,) if k in (0, 4) else (k, -k):
            for other in (0, 1):
                j = blk(other, kk)
                lo = HALF if other else 0
                cols = pl.ds(pl.multiple_of(j * BLK + lo, HALF), BLK - lo)
                part = jnp.dot(feats[:, cols], wg[c, j, lo:BLK], preferred_element_type=F32)
                if (kk, other) == (0, 0):
                    acc[c] = part
                else:
                    acc[c] += part

    def lend(ki):
        loads_once("feats")
        cols = pl.ds(pl.multiple_of(blk(1, ORDER[ki]) * BLK, BLK), HALF)
        send(("fx", ki), feats.at[:, cols], fnb.at[ki], xdev, 9)

    def product_lent(c, k):
        for kk in (k,) if k in (0, 4) else (k, -k):
            ki = ORDER.index(kk)
            if ki not in waited:
                waited.add(ki)
                arrive(("fx", ki), fnb.at[ki])
            part = jnp.dot(fnb[ki], wg[c, blk(0, kk), 0:HALF], preferred_element_type=F32)
            if kk == 0:
                accn[c] = part
            else:
                accn[c] += part
        if k == 4:
            ps[c] = accn[c].astype(BF16)
            send(("pn", c), ps.at[c], pr.at[c], xdev, 9)

    waited = set()

    def loads_once(name):
        if name not in waited:
            waited.add(name)
            loads[name].wait()

    factor_cache = []

    def factor_row():
        if not factor_cache:
            total = jnp.zeros((1, 1), F32)
            for j in range(16):
                digits = wg[0, j, BLK : BLK + 16].astype(F32)
                total = total + (16 * digits[0:1, 0:1] + digits[0:1, 128:129])
            factor_cache.append(jnp.where(live, LOSS_GAIN / (tok_count * total), 0.0))
        return factor_cache[0]

    def scaled(c):
        loads_once("targs")
        arrive(("pn", c), pr.at[c])
        err = acc[c] + pr[c].astype(F32) - targs[:, c * COLS : (c + 1) * COLS].astype(F32)
        st[c] = (err.T * factor_row()).astype(BF16)

    def lend_scaled(c):
        send(("sn", c), st.at[c], stn.at[c], xdev, 9)

    def scatter_span(c, name):
        if name == "b":
            return 0, COLS
        return (0, X_PART[c]) if name == "x" else (X_PART[c], COLS - X_PART[c])

    def share(c, name, k):
        lo, n = scatter_span(c, "x" if name == "c" else name)
        start = blk(name in ("n", "c"), k) * BLK + (0 if name == "b" else HALF)
        cols = pl.ds(pl.multiple_of(start, HALF), HALF)
        val = jnp.dot(st[c, lo : lo + n], feats[:, cols], preferred_element_type=F32)
        if name == "b":
            val = val + jnp.dot(stn[c], fnb[ORDER.index(k)], preferred_element_type=F32)
        return val

    def scatter_cross(c, ki):
        k, n = ORDER[ki], X_PART[c]
        xs[c, ki, 0:n] = share(c, "c", k).astype(BF16)
        send(("rx", c, k), xs.at[c, ki, pl.ds(0, n)], xr.at[c, ki, pl.ds(0, n)], xdev, 4 + c)

    def crossed(c, k, val):
        ki, n = ORDER.index(k), X_PART[c]
        arrive(("rx", c, k), xr.at[c, ki, pl.ds(0, n)])
        return val + xr[c, ki, 0:n].astype(F32)

    def scatter_first(c, name):
        lo, n = scatter_span(c, name)
        col = COLUMN[name]
        if name == "b":
            arrive(("sn", c), stn.at[c])
        val = share(c, name, 4)
        if name == "x":
            val = crossed(c, 4, val)
        z0[c, col, lo : lo + n] = val.astype(BF16)
        group = 6 + c if name == "b" else 4 + c
        for d in (1, -1):
            hlo, hn = part_of(lo, n, d)
            src, dst = z0.at[c, col, pl.ds(hlo, hn)], zr.at[c, lane(d, 1, col), pl.ds(hlo, hn)]
            send(("r", c, d, 1, name), src, dst, zdev[d], group)

    def lane(d, s, col):
        return (16 + (s - 1) * 2 if col == 2 else (s - 1) * 4 + col * 2) + (1 - d) // 2

    def scatter_step(c, s, name, d):
        lo, n = scatter_span(c, name)
        col = COLUMN[name]
        at = lane(d, s, col)
        k = d * (4 - s)
        val = share(c, name, k)
        if name == "x":
            val = crossed(c, k, val)
        if s == 1:
            hlo, hn = part_of(lo, n, d)
            olo, on = part_of(lo, n, -d)
            arrive(("r", c, d, s, name), zr.at[c, at, pl.ds(hlo, hn)])
            zr[c, at, olo : olo + on] = val[olo - lo : olo - lo + on].astype(BF16)
            got = zr[c, at, hlo : hlo + hn].astype(F32)
            zr[c, at, hlo : hlo + hn] = (val[hlo - lo : hlo - lo + hn] + got).astype(BF16)
        else:
            arrive(("r", c, d, s, name), zr.at[c, at, pl.ds(lo, n)])
            zr[c, at, lo : lo + n] = (val + zr[c, at, lo : lo + n].astype(F32)).astype(BF16)
        key = ("r", c, d, s + 1, name) if s < 3 else ("r", c, 4, name)
        send(key, zr.at[c, at, pl.ds(lo, n)], zr.at[c, lane(d, s + 1, col), pl.ds(lo, n)], zdev[d], (6 if col == 2 else 4) + c)

    def scatter_last(c, name):
        lo, n = scatter_span(c, name)
        col = COLUMN[name]
        val = share(c, name, 0)
        if name == "x":
            val = crossed(c, 0, val)
        arrive(("r", c, 4, name), zr.at[c, pl.ds(lane(1, 4, col), 2), pl.ds(lo, n)])
        for d in (1, -1):
            val = val + zr[c, lane(d, 4, col), lo : lo + n].astype(F32)
        if name == "n":
            fxs[c, 0:n] = val.astype(BF16)
            send(("fin", c), fxs.at[c, pl.ds(0, n)], fxr.at[c, pl.ds(0, n)], xdev, 4 + c)
        elif name == "b":
            gt[c, :, 0:HALF] = val
        else:
            gt[c, lo : lo + n, HALF:] = val

    def finish(c):
        lo, n = scatter_span(c, "n")
        if n:
            arrive(("fin", c), fxr.at[c, pl.ds(0, n)])
            gt[c, lo : lo + n, HALF:] += fxr[c, 0:n].astype(F32)
        store(gt.at[c], grad_hbm.at[c])

    stores = []

    def store(src, dst):
        copy = pltpu.make_async_copy(src, dst, store_sem.at[len(stores)])
        copy.start()
        stores.append(copy)

    nb8 = WIDTH // 8 // BLOCK_WIDTH

    def encode():
        loads["exps"].wait()
        loads["pg"].wait()
        signs = sign_table()
        inv = jnp.right_shift(8, exps_ref[...]).astype(F32) * 0.125
        scale = jnp.left_shift(1, exps_ref[...]).astype(F32)
        for p in range(8):
            base = p * nb8
            rows = jnp.concatenate(
                [pg[:, (base + b) * BLOCK_WIDTH : (base + b + 1) * BLOCK_WIDTH] for b in range(nb8)], axis=0
            )
            turned = rotate(rows, signs)
            for b in range(nb8):
                at = slice(b * BLOCK_WIDTH, (b + 1) * BLOCK_WIDTH)
                val = turned[b * 16 : (b + 1) * 16] * inv[:, base + b : base + b + 1]
                enc[p, :, at] = jnp.clip(val, -1.0, 1.0).astype(BF16)
                scl[p, :, at] = jnp.broadcast_to(scale[:, base + b : base + b + 1], (16, BLOCK_WIDTH))
        for k in range(1, 8):
            p = lax.rem(g + k, 8)
            send("enc", enc.at[p], landed.at[k - 1], (xh * 8 + p, f), 8)

    def partial_sum():
        arrive("enc", landed.at[pl.ds(0, 7)])
        total = enc[g].astype(F32)
        for k in range(1, 8):
            total = total + landed[k - 1].astype(F32)
        par_s[...] = total.astype(BF16)
        send("par", par_s, landed.at[7], ((1 - xh) * 8 + g, f), 8)

    def decode():
        arrive("par", landed.at[7])
        val = (par_s[...].astype(F32) + landed[7].astype(F32)) * (1.0 / REPLICAS) * scl[g]
        rows = jnp.concatenate([val[:, b * BLOCK_WIDTH : (b + 1) * BLOCK_WIDTH] for b in range(nb8)], axis=0)
        turned = rotate(rows, sign_table()).astype(BF16)
        mine = pl.ds(pl.multiple_of(g * 1024, 1024), 1024)
        dlt[:, mine] = jnp.concatenate([turned[b * 16 : (b + 1) * 16] for b in range(nb8)], axis=1)
        for k in range(1, 8):
            send("dlt", dlt.at[:, mine], dlt.at[:, mine], (xh * 8 + lax.rem(g + k, 8), f), 8)

    def update():
        arrive("dlt", landed.at[pl.ds(0, 7)])
        store(dlt, delta_hbm)

    steps = {
        "gs": gather_start,
        "gc": gather_cross,
        "gf": gather_forward,
        "gp": product,
        "fx": lend,
        "gq": product_lent,
        "ss": lend_scaled,
        "sc": scaled,
        "rc": scatter_cross,
        "rf": scatter_first,
        "rs": scatter_step,
        "rl": scatter_last,
        "fin": finish,
        "enc": encode,
        "par": partial_sum,
        "dec": decode,
        "upd": update,
    }
    for step in PLAN:
        steps[step[0]](*step[1:])
    assert len(slots) == N_SLOTS, len(slots)

    for c in range(CHUNKS):
        lo, n = gather_span(c, "o")
        sent(c, wg.at[c, pl.ds(0, 15), pl.ds(lo, n)])
        sent(2 + c, wg.at[c, pl.ds(0, 7), pl.ds(0, HALF)])
        sent(4 + c, zr.at[c, pl.ds(0, 15)])
        sent(6 + c, zr.at[c, pl.ds(0, 7)])
    sent(8, landed)
    sent(9, zr.at[0, pl.ds(0, 24)])
    for copy in stores:
        copy.wait()


def finish_kernel(gt_hbm, delta_hbm, params_hbm, moment_hbm, grad_hbm, newp_hbm, newm_hbm, gt, dlt, params, moment, out, newp, newm, load_sem, store_sem):
    loads = [
        pltpu.make_async_copy(gt_hbm.at[c], gt.at[c], load_sem.at[c]) for c in range(CHUNKS)
    ] + [
        pltpu.make_async_copy(delta_hbm, dlt, load_sem.at[CHUNKS]),
        pltpu.make_async_copy(params_hbm, params, load_sem.at[CHUNKS + 1]),
        pltpu.make_async_copy(moment_hbm, moment, load_sem.at[CHUNKS + 2]),
    ]
    for copy in loads:
        copy.start()
    stores = []

    def store(src, dst):
        copy = pltpu.make_async_copy(src, dst, store_sem.at[len(stores)])
        copy.start()
        stores.append(copy)

    for c in range(CHUNKS):
        loads[c].wait()
        out[:, c * COLS : (c + 1) * COLS] = gt[c].T
    store(out, grad_hbm.at[0])
    for copy in loads[CHUNKS:]:
        copy.wait()
    delta = dlt[...].astype(F32)
    new = MOMENTUM * moment[...] + delta
    newm[...] = new
    store(newm, newm_hbm)
    newp[...] = params[...] - OUTER_RATE * (delta + MOMENTUM * new)
    store(newp, newp_hbm)
    for copy in stores:
        copy.wait()


def on_device(features, targets, value_weight, segment_ids, traj_counts, pseudo_grad, block_exps, outer_params, outer_moment):
    hbm = pl.BlockSpec(memory_space=pl.ANY)
    xmax = max(X_PART)
    zmax = COLS - min(X_PART)
    out = pl.pallas_call(
        kernel,
        out_shape=(
            jax.ShapeDtypeStruct((CHUNKS, COLS, BLK), F32),
            jax.ShapeDtypeStruct((16, WIDTH), BF16),
        ),
        in_specs=[hbm] * 7,
        out_specs=(hbm, hbm),
        scratch_shapes=[
            pltpu.VMEM((TOK, WIDTH), BF16),
            pltpu.VMEM((TOK, 2 * COLS), BF16),
            pltpu.VMEM((CHUNKS, 16, BLK + EXTRA, COLS), BF16),
            pltpu.VMEM((CHUNKS, TOK, COLS), F32),
            pltpu.VMEM((CHUNKS, COLS, TOK), BF16),
            pltpu.VMEM((8, TOK, HALF), BF16),
            pltpu.VMEM((CHUNKS, TOK, COLS), F32),
            pltpu.VMEM((CHUNKS, TOK, COLS), BF16),
            pltpu.VMEM((CHUNKS, TOK, COLS), BF16),
            pltpu.VMEM((CHUNKS, COLS, TOK), BF16),
            pltpu.VMEM((CHUNKS, 8, xmax, HALF), BF16),
            pltpu.VMEM((CHUNKS, 8, xmax, HALF), BF16),
            pltpu.VMEM((CHUNKS, 3, COLS, HALF), BF16),
            pltpu.VMEM((CHUNKS, 24, COLS, HALF), BF16),
            pltpu.VMEM((CHUNKS, zmax, HALF), BF16),
            pltpu.VMEM((CHUNKS, zmax, HALF), BF16),
            pltpu.VMEM((CHUNKS, COLS, BLK), F32),
            pltpu.VMEM((CHUNKS, BLK, COLS), F32),
            pltpu.VMEM((16, WIDTH), F32),
            pltpu.VMEM((8, 16, 1024), F32),
            pltpu.VMEM((8, 16, 1024), BF16),
            pltpu.VMEM((15, 16, 1024), BF16),
            pltpu.VMEM((16, 1024), BF16),
            pltpu.VMEM((16, WIDTH), BF16),
            pltpu.VMEM((1, TOK), jnp.int32),
            pltpu.VMEM((1, 8), jnp.int32),
            pltpu.VMEM((16, WIDTH // BLOCK_WIDTH), jnp.int32),
            pltpu.SemaphoreType.DMA((CHUNKS + 6,)),
            pltpu.SemaphoreType.DMA((3,)),
            pltpu.SemaphoreType.DMA((10,)),
            pltpu.SemaphoreType.DMA((N_SLOTS,)),
        ],
        compiler_params=pltpu.CompilerParams(
            collective_id=0, has_side_effects=True, vmem_limit_bytes=56 * 2**20
        ),
    )(features, targets, value_weight, segment_ids, traj_counts, pseudo_grad, block_exps)
    wide = pltpu.VMEM((16, WIDTH), F32)
    return pl.pallas_call(
        finish_kernel,
        out_shape=(
            jax.ShapeDtypeStruct((1, BLK, CHUNKS * COLS), F32),
            jax.ShapeDtypeStruct((16, WIDTH), F32),
            jax.ShapeDtypeStruct((16, WIDTH), F32),
        ),
        in_specs=[hbm] * 4,
        out_specs=(hbm,) * 3,
        scratch_shapes=[
            pltpu.VMEM((CHUNKS, COLS, BLK), F32),
            pltpu.VMEM((16, WIDTH), BF16),
            wide,
            wide,
            pltpu.VMEM((BLK, CHUNKS * COLS), F32),
            wide,
            wide,
            pltpu.SemaphoreType.DMA((CHUNKS + 3,)),
            pltpu.SemaphoreType.DMA((3,)),
        ],
        compiler_params=pltpu.CompilerParams(vmem_limit_bytes=60 * 2**20),
    )(*out, outer_params, outer_moment)


def solution(mesh):
    return jax.shard_map(
        on_device,
        mesh=mesh,
        in_specs=(
            P("rep", "fsdp", None),
            P("rep", "fsdp", None),
            P("rep", "fsdp", None),
            P("rep", "fsdp"),
            P("rep", "fsdp"),
            P("rep", "fsdp", None),
            P("fsdp", None),
            P("fsdp", None),
            P("fsdp", None),
        ),
        out_specs=(P("rep", "fsdp", None), P("fsdp", None), P("fsdp", None)),
        check_vma=False,
    )
```

```python
import functools
import math

import jax
import jax.numpy as jnp
from jax import lax
from jax.experimental import pallas as pl
from jax.experimental.pallas import tpu as pltpu
from jax.sharding import PartitionSpec as P

MESH = pl.DeviceIdType.MESH
BLOCK_WIDTH = 128
MOMENTUM = 0.9
OUTER_RATE = 0.7
LOSS_GAIN = 4096.0
REPLICAS = 16
NZ = 8
BLK = 512
TOK = 512
WIDTH = 8192
COLS = 256
HALF = 256
CHUNKS = 2
PIECES = 2
N_SLOTS = 124
EXTRA = 32
X_ROWS = (HALF, HALF)
X_PART = (64, 256)
ORDER = (4, 3, -3, 2, -2, 1, -1, 0)
COLUMN = {"o": 0, "x": 0, "n": 1, "b": 2}
F32 = jnp.float32
BF16 = jnp.bfloat16
PLAN = (
    ("gs", 0), ("gb", 0), ("fx", 0), ("gc", 0),
    ("gp", 0, 0), ("gf", 0, 1, "o", -1), ("gf", 0, 1, "o", 1), ("enc",),
    ("fx", 1), ("gf", 0, 1, "x", 1), ("gf", 0, 1, "x", -1), ("gf", 0, 1, "n", 1),
    ("gf", 0, 1, "n", -1), ("gp", 0, 1), ("fx", 2), ("par",),
    ("gf", 0, 2, "o", 1), ("gf", 0, 2, "o", -1), ("gf", 0, 2, "x", 1), ("gf", 0, 2, "x", -1),
    ("fx", 3), ("dec",), ("gf", 0, 2, "n", -1), ("gf", 0, 2, "n", 1),
    ("gp", 0, 2), ("gf", 0, 3, "o", 1), ("gf", 0, 3, "o", -1), ("fx", 4),
    ("gs", 1), ("upd",), ("gf", 0, 3, "x", -1), ("gf", 0, 3, "x", 1),
    ("gf", 0, 3, "n", 1), ("gf", 0, 3, "n", -1), ("gp", 0, 3), ("gf", 0, 4, "o", 1),
    ("gf", 0, 4, "o", -1), ("gb", 1), ("fx", 5), ("gf", 1, 1, "o", 1),
    ("gf", 1, 1, "o", -1), ("gf", 0, 4, "x", 1), ("gf", 0, 4, "x", -1), ("gf", 0, 4, "n", 1),
    ("gf", 0, 4, "n", -1), ("gp", 0, 4), ("gc", 1), ("gp", 1, 0),
    ("fx", 6), ("gf", 1, 1, "x", 1), ("gf", 1, 1, "x", -1), ("gf", 1, 2, "o", 1),
    ("gf", 1, 2, "o", -1), ("fx", 7), ("gf", 1, 1, "n", 1), ("gf", 1, 1, "n", -1),
    ("gp", 1, 1), ("gf", 1, 2, "x", 1), ("gf", 1, 2, "x", -1), ("gf", 1, 3, "o", 1),
    ("gf", 1, 3, "o", -1), ("gq", 0, 0), ("gq", 0, 1), ("gq", 0, 2),
    ("gq", 0, 3), ("gq", 0, 4), ("gq", 1, 0), ("gq", 1, 1),
    ("gq", 1, 2), ("gf", 1, 2, "n", -1), ("gf", 1, 2, "n", 1), ("gp", 1, 2),
    ("gf", 1, 3, "x", 1), ("gf", 1, 3, "x", -1), ("gq", 1, 3), ("gf", 1, 4, "o", 1),
    ("gf", 1, 4, "o", -1), ("gf", 1, 3, "n", 1), ("gf", 1, 3, "n", -1), ("gp", 1, 3),
    ("sc", 0), ("ss", 0), ("rf", 0, "n"), ("gf", 1, 4, "x", -1),
    ("gf", 1, 4, "x", 1), ("gq", 1, 4), ("rf", 0, "o"), ("gf", 1, 4, "n", 1),
    ("gf", 1, 4, "n", -1), ("gp", 1, 4), ("rs", 0, 1, "n", 1), ("rs", 0, 1, "n", -1),
    ("rs", 0, 1, "o", 1), ("rs", 0, 1, "o", -1), ("rf", 0, "b"), ("rs", 0, 2, "n", 1),
    ("rs", 0, 2, "n", -1), ("rc", 0, 0), ("rc", 0, 1), ("rs", 0, 2, "o", 1),
    ("rs", 0, 2, "o", -1), ("rc", 0, 2), ("rc", 0, 3), ("rs", 0, 1, "b", 1),
    ("rs", 0, 1, "b", -1), ("rc", 0, 4), ("rc", 0, 5), ("sc", 1),
    ("rc", 0, 6), ("ss", 1), ("rs", 0, 3, "n", 1), ("rs", 0, 3, "n", -1),
    ("rf", 0, "x"), ("rs", 0, 3, "o", 1), ("rs", 0, 3, "o", -1), ("rs", 0, 2, "b", 1),
    ("rs", 0, 2, "b", -1), ("rc", 1, 0), ("rl", 0, "n"), ("rs", 0, 1, "x", -1),
    ("rs", 0, 1, "x", 1), ("rf", 1, "b"), ("rl", 0, "o"), ("rc", 1, 1),
    ("rf", 1, "x"), ("rs", 0, 3, "b", 1), ("rs", 0, 3, "b", -1), ("rc", 1, 2),
    ("rs", 0, 2, "x", 1), ("rs", 0, 2, "x", -1), ("rs", 1, 1, "b", 1), ("rs", 1, 1, "b", -1),
    ("rc", 1, 3), ("rs", 1, 1, "x", 1), ("rc", 1, 4), ("rl", 0, "b"),
    ("rs", 0, 3, "x", 1), ("rs", 0, 3, "x", -1), ("rs", 1, 1, "x", -1), ("rc", 1, 5),
    ("rs", 1, 2, "b", 1), ("rs", 1, 2, "b", -1), ("rc", 1, 6), ("rs", 1, 2, "x", 1),
    ("rs", 1, 2, "x", -1), ("rc", 1, 7), ("rs", 1, 3, "b", 1), ("rs", 1, 3, "b", -1),
    ("rc", 0, 7), ("rs", 1, 3, "x", 1), ("rs", 1, 3, "x", -1), ("rl", 0, "x"),
    ("fin", 0), ("rl", 1, "b"), ("rl", 1, "x"), ("fin", 1),
)


def sign_table():
    i = lax.broadcasted_iota(jnp.int32, (BLOCK_WIDTH, BLOCK_WIDTH), 0)
    j = lax.broadcasted_iota(jnp.int32, (BLOCK_WIDTH, BLOCK_WIDTH), 1)
    v = jnp.bitwise_and(i, j)
    for shift in (4, 2, 1):
        v = jnp.bitwise_xor(v, jnp.right_shift(v, shift))
    return (1 - 2 * jnp.bitwise_and(v, 1)).astype(F32).astype(BF16)


def rotate(rows, signs):
    hi = rows.astype(BF16)
    rest = rows - hi.astype(F32)
    mid = rest.astype(BF16)
    low = (rest - mid.astype(F32)).astype(BF16)
    total = jnp.dot(low, signs, preferred_element_type=F32)
    total = total + jnp.dot(mid, signs, preferred_element_type=F32)
    total = total + jnp.dot(hi, signs, preferred_element_type=F32)
    return total * (1.0 / math.sqrt(BLOCK_WIDTH))


def kernel(
    feats_hbm, targs_hbm, weight_hbm, seg_hbm, counts_hbm, pg_hbm, exps_hbm,
    grad_hbm, delta_hbm,
    feats, targs, wg, acc, st, fnb, accn, ps, pr, stn, xs, xr, z0, zr, fxs, fxr, gt, outw,
    pg, scl, enc, landed, par_s, dlt,
    seg_ref, counts_ref, exps_ref, load_sem, store_sem, ss, rs,
):
    r, f = lax.axis_index("rep"), lax.axis_index("fsdp")
    x, z = lax.div(f, NZ), lax.rem(f, NZ)
    xh, g = lax.div(r, 8), lax.rem(r, 8)

    def zz(k):
        return lax.rem(z + (k % NZ), NZ)

    def blk(other, k):
        return ((1 - x) if other else x) * NZ + zz(k)

    zdev = {1: (r, blk(0, 1)), -1: (r, blk(0, -1))}
    xdev = (r, blk(1, 0))
    slots = {}

    def slot(key):
        return rs.at[slots.setdefault(key, len(slots))]

    def send(key, src, dst, target, group):
        pltpu.make_async_remote_copy(
            src_ref=src, dst_ref=dst, send_sem=ss.at[group], recv_sem=slot(key), device_id=target, device_id_type=MESH
        ).start()

    def arrive(key, ref):
        pltpu.make_async_copy(ref, ref, slot(key)).wait()

    def sent(group, ref):
        pltpu.make_async_copy(ref, ref, ss.at[group]).wait()

    loads = {}

    def load(name, src, dst):
        loads[name] = pltpu.make_async_copy(src, dst, load_sem.at[len(loads)])
        loads[name].start()

    for c in range(CHUNKS):
        load(f"w{c}", weight_hbm.at[0, :, pl.ds(c * COLS, COLS)], wg.at[c, f, pl.ds(0, BLK)])
    load("seg", seg_hbm, seg_ref)
    load("counts", counts_hbm, counts_ref)
    load("exps", exps_hbm, exps_ref)
    load("pg", pg_hbm.at[0], pg)
    load("feats", feats_hbm.at[0], feats)
    load("targs", targs_hbm.at[0], targs)

    barrier = pltpu.get_barrier_semaphore()
    for target in (zdev[1], zdev[-1], xdev):
        pl.semaphore_signal(barrier, inc=1, device_id=target, device_id_type=MESH)
    for k in range(1, 8):
        pl.semaphore_signal(barrier, inc=1, device_id=(xh * 8 + lax.rem(g + k, 8), f), device_id_type=MESH)
    pl.semaphore_signal(barrier, inc=1, device_id=((1 - xh) * 8 + g, f), device_id_type=MESH)

    loads["seg"].wait()
    loads["counts"].wait()
    seg = seg_ref[...]
    live = seg >= 0
    live_here = jnp.sum(live.astype(F32), axis=1, keepdims=True)
    tens = jnp.floor(live_here * (1.0 / 16))
    wg[0, f, BLK:, 0:128] = jnp.broadcast_to(tens, (EXTRA, 128)).astype(BF16)
    wg[0, f, BLK:, 128:] = jnp.broadcast_to(live_here - 16 * tens, (EXTRA, COLS - 128)).astype(BF16)
    tok_count = jnp.zeros((1, TOK), F32)
    counts = counts_ref[...].astype(F32)
    for s in range(8):
        tok_count = tok_count + jnp.where(seg == s, counts[:, s : s + 1], 0.0)
    tok_count = jnp.where(live, tok_count, 1.0)
    pl.semaphore_wait(barrier, 11)

    def gather_push(key, c, j, lo, n, target):
        ref = wg.at[c, j, pl.ds(lo, n)]
        send(key, ref, ref, target, 2 + c if lo < HALF else c)

    def gather_span(c, name):
        return (0, X_ROWS[c]) if name == "x" else (X_ROWS[c], BLK - X_ROWS[c] + (0 if c else EXTRA))

    def part_of(lo, n, d):
        return (lo, n // 2) if d == 1 else (lo + n // 2, n // 2)

    def gather_start(c):
        loads_once(f"w{c}")
        lo, n = gather_span(c, "o")
        gather_push(("nb", c), c, blk(0, 0), lo, n, xdev)
        for d in (1, -1):
            gather_push(("g", c, d, 1, "o"), c, blk(0, 0), lo, n, zdev[d])

    def gather_half(c):
        loads_once(f"w{c}")
        lo, n = gather_span(c, "x")
        for d in (1, -1):
            gather_push(("g", c, d, 1, "x"), c, blk(0, 0), lo, n, zdev[d])

    def gather_cross(c):
        lo, n = gather_span(c, "n")
        arrive(("nb", c), wg.at[c, blk(1, 0), pl.ds(lo, n)])
        for d in (1, -1):
            gather_push(("g", c, d, 1, "n"), c, blk(1, 0), lo, n, zdev[d])

    def gather_forward(c, s, name, d):
        j = blk(name == "n", -d * s)
        lo, n = gather_span(c, name)
        half = part_of(lo, n, d)
        arrive(("g", c, d, s, name), wg.at[c, j, pl.ds(*((lo, n) if s < 4 else half))])
        if s < 4:
            at = (lo, n) if s < 3 else half
            gather_push(("g", c, d, s + 1, name), c, j, *at, zdev[d])

    def product(c, k):
        if k == 0:
            loads_once("feats")
        for kk in (k,) if k in (0, 4) else (k, -k):
            for other in (0, 1):
                j = blk(other, kk)
                lo = HALF if other else 0
                cols = pl.ds(pl.multiple_of(j * BLK + lo, HALF), BLK - lo)
                part = jnp.dot(feats[:, cols], wg[c, j, lo:BLK], preferred_element_type=F32)
                if (kk, other) == (0, 0):
                    acc[c] = part
                else:
                    acc[c] += part

    def lend(ki):
        loads_once("feats")
        cols = pl.ds(pl.multiple_of(blk(1, ORDER[ki]) * BLK, BLK), HALF)
        send(("fx", ki), feats.at[:, cols], fnb.at[ki], xdev, 9)

    def product_lent(c, k):
        for kk in (k,) if k in (0, 4) else (k, -k):
            ki = ORDER.index(kk)
            if ki not in waited:
                waited.add(ki)
                arrive(("fx", ki), fnb.at[ki])
            part = jnp.dot(fnb[ki], wg[c, blk(0, kk), 0:HALF], preferred_element_type=F32)
            if kk == 0:
                accn[c] = part
            else:
                accn[c] += part
        if k == 4:
            ps[c] = accn[c].astype(BF16)
            send(("pn", c), ps.at[c], pr.at[c], xdev, 9)

    waited = set()

    def loads_once(name):
        if name not in waited:
            waited.add(name)
            loads[name].wait()

    factor_cache = []

    def factor_row():
        if not factor_cache:
            total = jnp.zeros((1, 1), F32)
            for j in range(16):
                digits = wg[0, j, BLK : BLK + 16].astype(F32)
                total = total + (16 * digits[0:1, 0:1] + digits[0:1, 128:129])
            factor_cache.append(jnp.where(live, LOSS_GAIN / (tok_count * total), 0.0))
        return factor_cache[0]

    def scaled(c):
        loads_once("targs")
        arrive(("pn", c), pr.at[c])
        err = acc[c] + pr[c].astype(F32) - targs[:, c * COLS : (c + 1) * COLS].astype(F32)
        st[c] = (err.T * factor_row()).astype(BF16)

    def lend_scaled(c):
        send(("sn", c), st.at[c], stn.at[c], xdev, 9)

    def scatter_span(c, name):
        if name == "b":
            return 0, COLS
        return (0, X_PART[c]) if name == "x" else (X_PART[c], COLS - X_PART[c])

    def share(c, name, k):
        lo, n = scatter_span(c, "x" if name == "c" else name)
        start = blk(name in ("n", "c"), k) * BLK + (0 if name == "b" else HALF)
        cols = pl.ds(pl.multiple_of(start, HALF), HALF)
        val = jnp.dot(st[c, lo : lo + n], feats[:, cols], preferred_element_type=F32)
        if name == "b":
            val = val + jnp.dot(stn[c], fnb[ORDER.index(k)], preferred_element_type=F32)
        return val

    def scatter_cross(c, ki):
        k, n = ORDER[ki], X_PART[c]
        xs[c, ki, 0:n] = share(c, "c", k).astype(BF16)
        send(("rx", c, k), xs.at[c, ki, pl.ds(0, n)], xr.at[c, ki, pl.ds(0, n)], xdev, 4 + c)

    def crossed(c, k, val):
        ki, n = ORDER.index(k), X_PART[c]
        arrive(("rx", c, k), xr.at[c, ki, pl.ds(0, n)])
        return val + xr[c, ki, 0:n].astype(F32)

    def scatter_first(c, name):
        lo, n = scatter_span(c, name)
        col = COLUMN[name]
        if name == "b":
            arrive(("sn", c), stn.at[c])
        val = share(c, name, 4)
        if name == "x":
            val = crossed(c, 4, val)
        z0[c, col, lo : lo + n] = val.astype(BF16)
        group = 6 + c if name == "b" else 4 + c
        for d in (1, -1):
            hlo, hn = part_of(lo, n, d)
            src, dst = z0.at[c, col, pl.ds(hlo, hn)], zr.at[c, lane(d, 1, col), pl.ds(hlo, hn)]
            send(("r", c, d, 1, name), src, dst, zdev[d], group)

    def lane(d, s, col):
        return (16 + (s - 1) * 2 if col == 2 else (s - 1) * 4 + col * 2) + (1 - d) // 2

    def scatter_step(c, s, name, d):
        lo, n = scatter_span(c, name)
        col = COLUMN[name]
        at = lane(d, s, col)
        k = d * (4 - s)
        val = share(c, name, k)
        if name == "x":
            val = crossed(c, k, val)
        if s == 1:
            hlo, hn = part_of(lo, n, d)
            olo, on = part_of(lo, n, -d)
            arrive(("r", c, d, s, name), zr.at[c, at, pl.ds(hlo, hn)])
            zr[c, at, olo : olo + on] = val[olo - lo : olo - lo + on].astype(BF16)
            got = zr[c, at, hlo : hlo + hn].astype(F32)
            zr[c, at, hlo : hlo + hn] = (val[hlo - lo : hlo - lo + hn] + got).astype(BF16)
        else:
            arrive(("r", c, d, s, name), zr.at[c, at, pl.ds(lo, n)])
            zr[c, at, lo : lo + n] = (val + zr[c, at, lo : lo + n].astype(F32)).astype(BF16)
        key = ("r", c, d, s + 1, name) if s < 3 else ("r", c, 4, name)
        send(key, zr.at[c, at, pl.ds(lo, n)], zr.at[c, lane(d, s + 1, col), pl.ds(lo, n)], zdev[d], (6 if col == 2 else 4) + c)

    def scatter_last(c, name):
        lo, n = scatter_span(c, name)
        col = COLUMN[name]
        val = share(c, name, 0)
        if name == "x":
            val = crossed(c, 0, val)
        arrive(("r", c, 4, name), zr.at[c, pl.ds(lane(1, 4, col), 2), pl.ds(lo, n)])
        for d in (1, -1):
            val = val + zr[c, lane(d, 4, col), lo : lo + n].astype(F32)
        if name == "n":
            fxs[c, 0:n] = val.astype(BF16)
            send(("fin", c), fxs.at[c, pl.ds(0, n)], fxr.at[c, pl.ds(0, n)], xdev, 4 + c)
        elif name == "b":
            gt[c, :, 0:HALF] = val
        else:
            gt[c, lo : lo + n, HALF:] = val

    def finish(c):
        lo, n = scatter_span(c, "n")
        if n:
            arrive(("fin", c), fxr.at[c, pl.ds(0, n)])
            gt[c, lo : lo + n, HALF:] += fxr[c, 0:n].astype(F32)
        store(gt.at[c], grad_hbm.at[c])

    stores = []

    def store(src, dst):
        copy = pltpu.make_async_copy(src, dst, store_sem.at[len(stores)])
        copy.start()
        stores.append(copy)

    nb8 = WIDTH // 8 // BLOCK_WIDTH

    def encode():
        loads["exps"].wait()
        loads["pg"].wait()
        signs = sign_table()
        inv = jnp.right_shift(8, exps_ref[...]).astype(F32) * 0.125
        scale = jnp.left_shift(1, exps_ref[...]).astype(F32)
        for p in range(8):
            base = p * nb8
            rows = jnp.concatenate(
                [pg[:, (base + b) * BLOCK_WIDTH : (base + b + 1) * BLOCK_WIDTH] for b in range(nb8)], axis=0
            )
            turned = rotate(rows, signs)
            for b in range(nb8):
                at = slice(b * BLOCK_WIDTH, (b + 1) * BLOCK_WIDTH)
                val = turned[b * 16 : (b + 1) * 16] * inv[:, base + b : base + b + 1]
                enc[p, :, at] = jnp.clip(val, -1.0, 1.0).astype(BF16)
                scl[p, :, at] = jnp.broadcast_to(scale[:, base + b : base + b + 1], (16, BLOCK_WIDTH))
        for k in range(1, 8):
            p = lax.rem(g + k, 8)
            send("enc", enc.at[p], landed.at[k - 1], (xh * 8 + p, f), 8)

    def partial_sum():
        arrive("enc", landed.at[pl.ds(0, 7)])
        total = enc[g].astype(F32)
        for k in range(1, 8):
            total = total + landed[k - 1].astype(F32)
        par_s[...] = total.astype(BF16)
        send("par", par_s, landed.at[7], ((1 - xh) * 8 + g, f), 8)

    def decode():
        arrive("par", landed.at[7])
        val = (par_s[...].astype(F32) + landed[7].astype(F32)) * (1.0 / REPLICAS) * scl[g]
        rows = jnp.concatenate([val[:, b * BLOCK_WIDTH : (b + 1) * BLOCK_WIDTH] for b in range(nb8)], axis=0)
        turned = rotate(rows, sign_table()).astype(BF16)
        mine = pl.ds(pl.multiple_of(g * 1024, 1024), 1024)
        dlt[:, mine] = jnp.concatenate([turned[b * 16 : (b + 1) * 16] for b in range(nb8)], axis=1)
        for k in range(1, 8):
            send("dlt", dlt.at[:, mine], dlt.at[:, mine], (xh * 8 + lax.rem(g + k, 8), f), 8)

    def update():
        arrive("dlt", landed.at[pl.ds(0, 7)])
        store(dlt, delta_hbm)

    steps = {
        "gs": gather_start,
        "gb": gather_half,
        "gc": gather_cross,
        "gf": gather_forward,
        "gp": product,
        "fx": lend,
        "gq": product_lent,
        "ss": lend_scaled,
        "sc": scaled,
        "rc": scatter_cross,
        "rf": scatter_first,
        "rs": scatter_step,
        "rl": scatter_last,
        "fin": finish,
        "enc": encode,
        "par": partial_sum,
        "dec": decode,
        "upd": update,
    }
    for step in PLAN:
        steps[step[0]](*step[1:])
    assert len(slots) == N_SLOTS, len(slots)

    for c in range(CHUNKS):
        lo, n = gather_span(c, "o")
        sent(c, wg.at[c, pl.ds(0, 15), pl.ds(lo, n)])
        sent(2 + c, wg.at[c, pl.ds(0, 7), pl.ds(0, HALF)])
        sent(4 + c, zr.at[c, pl.ds(0, 15)])
        sent(6 + c, zr.at[c, pl.ds(0, 7)])
    sent(8, landed)
    sent(9, zr.at[0, pl.ds(0, 24)])
    for copy in stores:
        copy.wait()


def finish_kernel(gt_hbm, delta_hbm, params_hbm, moment_hbm, grad_hbm, newp_hbm, newm_hbm, gt, dlt, params, moment, out, newp, newm, load_sem, store_sem):
    piece = BLK // PIECES
    loads = [
        pltpu.make_async_copy(gt_hbm.at[:, :, pl.ds(q * piece, piece)], gt.at[q], load_sem.at[q]) for q in range(PIECES)
    ] + [
        pltpu.make_async_copy(delta_hbm, dlt, load_sem.at[PIECES]),
        pltpu.make_async_copy(params_hbm, params, load_sem.at[PIECES + 1]),
        pltpu.make_async_copy(moment_hbm, moment, load_sem.at[PIECES + 2]),
    ]
    for copy in loads:
        copy.start()
    stores = []

    def store(src, dst):
        copy = pltpu.make_async_copy(src, dst, store_sem.at[len(stores)])
        copy.start()
        stores.append(copy)

    for q in range(PIECES):
        loads[q].wait()
        for c in range(CHUNKS):
            out[q * piece : (q + 1) * piece, c * COLS : (c + 1) * COLS] = gt[q, c].T
        store(out.at[pl.ds(q * piece, piece)], grad_hbm.at[0, pl.ds(q * piece, piece)])
    for copy in loads[PIECES:]:
        copy.wait()
    delta = dlt[...].astype(F32)
    new = MOMENTUM * moment[...] + delta
    newm[...] = new
    store(newm, newm_hbm)
    newp[...] = params[...] - OUTER_RATE * (delta + MOMENTUM * new)
    store(newp, newp_hbm)
    for copy in stores:
        copy.wait()


def on_device(features, targets, value_weight, segment_ids, traj_counts, pseudo_grad, block_exps, outer_params, outer_moment):
    hbm = pl.BlockSpec(memory_space=pl.ANY)
    xmax = max(X_PART)
    zmax = COLS - min(X_PART)
    out = pl.pallas_call(
        kernel,
        out_shape=(
            jax.ShapeDtypeStruct((CHUNKS, COLS, BLK), F32),
            jax.ShapeDtypeStruct((16, WIDTH), BF16),
        ),
        in_specs=[hbm] * 7,
        out_specs=(hbm, hbm),
        scratch_shapes=[
            pltpu.VMEM((TOK, WIDTH), BF16),
            pltpu.VMEM((TOK, 2 * COLS), BF16),
            pltpu.VMEM((CHUNKS, 16, BLK + EXTRA, COLS), BF16),
            pltpu.VMEM((CHUNKS, TOK, COLS), F32),
            pltpu.VMEM((CHUNKS, COLS, TOK), BF16),
            pltpu.VMEM((8, TOK, HALF), BF16),
            pltpu.VMEM((CHUNKS, TOK, COLS), F32),
            pltpu.VMEM((CHUNKS, TOK, COLS), BF16),
            pltpu.VMEM((CHUNKS, TOK, COLS), BF16),
            pltpu.VMEM((CHUNKS, COLS, TOK), BF16),
            pltpu.VMEM((CHUNKS, 8, xmax, HALF), BF16),
            pltpu.VMEM((CHUNKS, 8, xmax, HALF), BF16),
            pltpu.VMEM((CHUNKS, 3, COLS, HALF), BF16),
            pltpu.VMEM((CHUNKS, 24, COLS, HALF), BF16),
            pltpu.VMEM((CHUNKS, zmax, HALF), BF16),
            pltpu.VMEM((CHUNKS, zmax, HALF), BF16),
            pltpu.VMEM((CHUNKS, COLS, BLK), F32),
            pltpu.VMEM((CHUNKS, BLK, COLS), F32),
            pltpu.VMEM((16, WIDTH), F32),
            pltpu.VMEM((8, 16, 1024), F32),
            pltpu.VMEM((8, 16, 1024), BF16),
            pltpu.VMEM((15, 16, 1024), BF16),
            pltpu.VMEM((16, 1024), BF16),
            pltpu.VMEM((16, WIDTH), BF16),
            pltpu.VMEM((1, TOK), jnp.int32),
            pltpu.VMEM((1, 8), jnp.int32),
            pltpu.VMEM((16, WIDTH // BLOCK_WIDTH), jnp.int32),
            pltpu.SemaphoreType.DMA((CHUNKS + 6,)),
            pltpu.SemaphoreType.DMA((3,)),
            pltpu.SemaphoreType.DMA((10,)),
            pltpu.SemaphoreType.DMA((N_SLOTS,)),
        ],
        compiler_params=pltpu.CompilerParams(
            collective_id=0, has_side_effects=True, vmem_limit_bytes=56 * 2**20
        ),
    )(features, targets, value_weight, segment_ids, traj_counts, pseudo_grad, block_exps)
    wide = pltpu.VMEM((16, WIDTH), F32)
    return pl.pallas_call(
        finish_kernel,
        out_shape=(
            jax.ShapeDtypeStruct((1, BLK, CHUNKS * COLS), F32),
            jax.ShapeDtypeStruct((16, WIDTH), F32),
            jax.ShapeDtypeStruct((16, WIDTH), F32),
        ),
        in_specs=[hbm] * 4,
        out_specs=(hbm,) * 3,
        scratch_shapes=[
            pltpu.VMEM((PIECES, CHUNKS, COLS, BLK // PIECES), F32),
            pltpu.VMEM((16, WIDTH), BF16),
            wide,
            wide,
            pltpu.VMEM((BLK, CHUNKS * COLS), F32),
            wide,
            wide,
            pltpu.SemaphoreType.DMA((PIECES + 3,)),
            pltpu.SemaphoreType.DMA((PIECES + 2,)),
        ],
        compiler_params=pltpu.CompilerParams(vmem_limit_bytes=60 * 2**20),
    )(*out, outer_params, outer_moment)


def solution(mesh):
    return jax.shard_map(
        on_device,
        mesh=mesh,
        in_specs=(
            P("rep", "fsdp", None),
            P("rep", "fsdp", None),
            P("rep", "fsdp", None),
            P("rep", "fsdp"),
            P("rep", "fsdp"),
            P("rep", "fsdp", None),
            P("fsdp", None),
            P("fsdp", None),
            P("fsdp", None),
        ),
        out_specs=(P("rep", "fsdp", None), P("fsdp", None), P("fsdp", None)),
        check_vma=False,
    )
```

```python
import functools
import math

import jax
import jax.numpy as jnp
from jax import lax
from jax.experimental import pallas as pl
from jax.experimental.pallas import tpu as pltpu
from jax.sharding import PartitionSpec as P

MESH = pl.DeviceIdType.MESH
BLOCK_WIDTH = 128
MOMENTUM = 0.9
OUTER_RATE = 0.7
LOSS_GAIN = 4096.0
REPLICAS = 16
NZ = 8
BLK = 512
TOK = 512
WIDTH = 8192
COLS = 256
HALF = 256
CHUNKS = 2
N_SLOTS = 124
EXTRA = 32
X_ROWS = (HALF, HALF)
X_PART = (64, 256)
ORDER = (4, 3, -3, 2, -2, 1, -1, 0)
COLUMN = {"o": 0, "x": 0, "n": 1, "b": 2}
F32 = jnp.float32
BF16 = jnp.bfloat16
PLAN = (
    ("gs", 0), ("fx", 0), ("gc", 0), ("gp", 0, 0),
    ("gf", 0, 1, "o", 1), ("gf", 0, 1, "o", -1), ("enc",), ("fx", 1),
    ("gf", 0, 1, "x", 1), ("gf", 0, 1, "x", -1), ("gf", 0, 1, "n", 1), ("gf", 0, 1, "n", -1),
    ("gp", 0, 1), ("fx", 2), ("par",), ("gf", 0, 2, "o", 1),
    ("gf", 0, 2, "o", -1), ("gf", 0, 2, "x", 1), ("gf", 0, 2, "x", -1), ("fx", 3),
    ("dec",), ("gf", 0, 2, "n", 1), ("gf", 0, 2, "n", -1), ("gp", 0, 2),
    ("gf", 0, 3, "o", 1), ("gf", 0, 3, "o", -1), ("fx", 4), ("upd",),
    ("gf", 0, 3, "x", 1), ("gf", 0, 3, "x", -1), ("gf", 0, 3, "n", 1), ("gf", 0, 3, "n", -1),
    ("gp", 0, 3), ("fx", 5), ("gs", 1), ("gf", 0, 4, "o", 1),
    ("gf", 0, 4, "o", -1), ("gf", 0, 4, "x", 1), ("gf", 0, 4, "x", -1), ("gf", 0, 4, "n", 1),
    ("gf", 0, 4, "n", -1), ("gp", 0, 4), ("gf", 1, 1, "o", 1), ("gf", 1, 1, "o", -1),
    ("fx", 6), ("gf", 1, 1, "x", 1), ("gf", 1, 1, "x", -1), ("gc", 1),
    ("gp", 1, 0), ("gf", 1, 2, "o", 1), ("gf", 1, 2, "o", -1), ("fx", 7),
    ("gf", 1, 2, "x", 1), ("gf", 1, 2, "x", -1), ("gf", 1, 1, "n", 1), ("gf", 1, 1, "n", -1),
    ("gp", 1, 1), ("gf", 1, 3, "o", 1), ("gf", 1, 3, "o", -1), ("gq", 0, 0),
    ("gq", 0, 1), ("gq", 0, 2), ("gq", 0, 3), ("gq", 0, 4),
    ("gq", 1, 0), ("gf", 1, 3, "x", 1), ("gf", 1, 3, "x", -1), ("gq", 1, 1),
    ("gf", 1, 2, "n", 1), ("gf", 1, 2, "n", -1), ("gp", 1, 2), ("gq", 1, 2),
    ("gf", 1, 4, "o", 1), ("gf", 1, 4, "o", -1), ("gf", 1, 4, "x", 1), ("gf", 1, 4, "x", -1),
    ("sc", 0), ("ss", 0), ("rf", 0, "o"), ("rf", 0, "n"),
    ("gf", 1, 3, "n", 1), ("gf", 1, 3, "n", -1), ("gp", 1, 3), ("gq", 1, 3),
    ("rs", 0, 1, "o", 1), ("rs", 0, 1, "o", -1), ("rc", 0, 0), ("rc", 0, 1),
    ("rs", 0, 1, "n", 1), ("rs", 0, 1, "n", -1), ("rc", 0, 2), ("rc", 0, 3),
    ("gf", 1, 4, "n", 1), ("gf", 1, 4, "n", -1), ("gp", 1, 4), ("gq", 1, 4),
    ("rf", 0, "b"), ("rs", 0, 2, "o", 1), ("rs", 0, 2, "o", -1), ("rf", 0, "x"),
    ("rs", 0, 2, "n", 1), ("rs", 0, 2, "n", -1), ("rs", 0, 1, "b", 1), ("rs", 0, 1, "b", -1),
    ("rc", 0, 4), ("rc", 0, 5), ("rc", 0, 6), ("rc", 0, 7),
    ("rs", 0, 3, "o", 1), ("rs", 0, 3, "o", -1), ("rs", 0, 1, "x", 1), ("rs", 0, 1, "x", -1),
    ("sc", 1), ("ss", 1), ("rs", 0, 3, "n", 1), ("rs", 0, 3, "n", -1),
    ("rs", 0, 2, "b", 1), ("rs", 0, 2, "b", -1), ("rc", 1, 0), ("rl", 0, "o"),
    ("rs", 0, 2, "x", 1), ("rs", 0, 2, "x", -1), ("rc", 1, 1), ("rf", 1, "b"),
    ("rl", 0, "n"), ("rf", 1, "x"), ("rs", 0, 3, "b", 1), ("rs", 0, 3, "b", -1),
    ("rc", 1, 2), ("rs", 0, 3, "x", 1), ("rs", 0, 3, "x", -1), ("rs", 1, 1, "b", 1),
    ("rs", 1, 1, "b", -1), ("rc", 1, 3), ("rs", 1, 1, "x", 1), ("rc", 1, 4),
    ("rl", 0, "b"), ("rs", 1, 1, "x", -1), ("rl", 0, "x"), ("fin", 0),
    ("rc", 1, 5), ("rs", 1, 2, "b", 1), ("rs", 1, 2, "b", -1), ("rc", 1, 6),
    ("rs", 1, 2, "x", 1), ("rs", 1, 2, "x", -1), ("rc", 1, 7), ("rs", 1, 3, "b", 1),
    ("rs", 1, 3, "b", -1), ("rs", 1, 3, "x", 1), ("rs", 1, 3, "x", -1), ("rl", 1, "b"),
    ("rl", 1, "x"), ("fin", 1),
)


def sign_table():
    i = lax.broadcasted_iota(jnp.int32, (BLOCK_WIDTH, BLOCK_WIDTH), 0)
    j = lax.broadcasted_iota(jnp.int32, (BLOCK_WIDTH, BLOCK_WIDTH), 1)
    v = jnp.bitwise_and(i, j)
    for shift in (4, 2, 1):
        v = jnp.bitwise_xor(v, jnp.right_shift(v, shift))
    return (1 - 2 * jnp.bitwise_and(v, 1)).astype(F32).astype(BF16)


def rotate(rows, signs):
    hi = rows.astype(BF16)
    rest = rows - hi.astype(F32)
    mid = rest.astype(BF16)
    low = (rest - mid.astype(F32)).astype(BF16)
    total = jnp.dot(low, signs, preferred_element_type=F32)
    total = total + jnp.dot(mid, signs, preferred_element_type=F32)
    total = total + jnp.dot(hi, signs, preferred_element_type=F32)
    return total * (1.0 / math.sqrt(BLOCK_WIDTH))


def kernel(
    feats_hbm, targs_hbm, weight_hbm, seg_hbm, counts_hbm, pg_hbm, exps_hbm,
    grad_hbm, delta_hbm,
    feats, targs, wg, acc, st, fnb, accn, ps, pr, stn, xs, xr, z0, zr, fxs, fxr, gt, outw,
    pg, scl, enc, landed, par_s, dlt,
    seg_ref, counts_ref, exps_ref, load_sem, store_sem, ss, rs,
):
    r, f = lax.axis_index("rep"), lax.axis_index("fsdp")
    x, z = lax.div(f, NZ), lax.rem(f, NZ)
    xh, g = lax.div(r, 8), lax.rem(r, 8)

    def zz(k):
        return lax.rem(z + (k % NZ), NZ)

    def blk(other, k):
        return ((1 - x) if other else x) * NZ + zz(k)

    zdev = {1: (r, blk(0, 1)), -1: (r, blk(0, -1))}
    xdev = (r, blk(1, 0))
    slots = {}

    def slot(key):
        return rs.at[slots.setdefault(key, len(slots))]

    def send(key, src, dst, target, group):
        pltpu.make_async_remote_copy(
            src_ref=src, dst_ref=dst, send_sem=ss.at[group], recv_sem=slot(key), device_id=target, device_id_type=MESH
        ).start()

    def arrive(key, ref):
        pltpu.make_async_copy(ref, ref, slot(key)).wait()

    def sent(group, ref):
        pltpu.make_async_copy(ref, ref, ss.at[group]).wait()

    loads = {}

    def load(name, src, dst):
        loads[name] = pltpu.make_async_copy(src, dst, load_sem.at[len(loads)])
        loads[name].start()

    for c in range(CHUNKS):
        load(f"w{c}", weight_hbm.at[0, :, pl.ds(c * COLS, COLS)], wg.at[c, f, pl.ds(0, BLK)])
    load("seg", seg_hbm, seg_ref)
    load("counts", counts_hbm, counts_ref)
    load("exps", exps_hbm, exps_ref)
    load("pg", pg_hbm.at[0], pg)
    load("feats", feats_hbm.at[0], feats)
    load("targs", targs_hbm.at[0], targs)

    barrier = pltpu.get_barrier_semaphore()
    for target in (zdev[1], zdev[-1], xdev):
        pl.semaphore_signal(barrier, inc=1, device_id=target, device_id_type=MESH)
    for k in range(1, 8):
        pl.semaphore_signal(barrier, inc=1, device_id=(xh * 8 + lax.rem(g + k, 8), f), device_id_type=MESH)
    pl.semaphore_signal(barrier, inc=1, device_id=((1 - xh) * 8 + g, f), device_id_type=MESH)

    loads["seg"].wait()
    loads["counts"].wait()
    seg = seg_ref[...]
    live = seg >= 0
    live_here = jnp.sum(live.astype(F32), axis=1, keepdims=True)
    tens = jnp.floor(live_here * (1.0 / 16))
    wg[0, f, BLK:, 0:128] = jnp.broadcast_to(tens, (EXTRA, 128)).astype(BF16)
    wg[0, f, BLK:, 128:] = jnp.broadcast_to(live_here - 16 * tens, (EXTRA, COLS - 128)).astype(BF16)
    tok_count = jnp.zeros((1, TOK), F32)
    counts = counts_ref[...].astype(F32)
    for s in range(8):
        tok_count = tok_count + jnp.where(seg == s, counts[:, s : s + 1], 0.0)
    tok_count = jnp.where(live, tok_count, 1.0)
    pl.semaphore_wait(barrier, 11)

    def gather_push(key, c, j, lo, n, target):
        ref = wg.at[c, j, pl.ds(lo, n)]
        send(key, ref, ref, target, 2 + c if lo < HALF else c)

    def gather_span(c, name):
        return (0, X_ROWS[c]) if name == "x" else (X_ROWS[c], BLK - X_ROWS[c] + (0 if c else EXTRA))

    def part_of(lo, n, d):
        return (lo, n // 2) if d == 1 else (lo + n // 2, n // 2)

    def gather_start(c):
        loads[f"w{c}"].wait()
        own = blk(0, 0)
        lo, n = gather_span(c, "o")
        if n:
            gather_push(("nb", c), c, own, lo, n, xdev)
        for name in ("o", "x"):
            lo, n = gather_span(c, name)
            if n:
                for d in (1, -1):
                    gather_push(("g", c, d, 1, name), c, own, lo, n, zdev[d])

    def gather_cross(c):
        lo, n = gather_span(c, "n")
        arrive(("nb", c), wg.at[c, blk(1, 0), pl.ds(lo, n)])
        for d in (1, -1):
            gather_push(("g", c, d, 1, "n"), c, blk(1, 0), lo, n, zdev[d])

    def gather_forward(c, s, name, d):
        j = blk(name == "n", -d * s)
        lo, n = gather_span(c, name)
        half = part_of(lo, n, d)
        arrive(("g", c, d, s, name), wg.at[c, j, pl.ds(*((lo, n) if s < 4 else half))])
        if s < 4:
            at = (lo, n) if s < 3 else half
            gather_push(("g", c, d, s + 1, name), c, j, *at, zdev[d])

    def product(c, k):
        if k == 0:
            loads_once("feats")
        for kk in (k,) if k in (0, 4) else (k, -k):
            for other in (0, 1):
                j = blk(other, kk)
                lo = HALF if other else 0
                cols = pl.ds(pl.multiple_of(j * BLK + lo, HALF), BLK - lo)
                part = jnp.dot(feats[:, cols], wg[c, j, lo:BLK], preferred_element_type=F32)
                if (kk, other) == (0, 0):
                    acc[c] = part
                else:
                    acc[c] += part

    def lend(ki):
        cols = pl.ds(pl.multiple_of(blk(1, ORDER[ki]) * BLK, BLK), HALF)
        send(("fx", ki), feats_hbm.at[0, :, cols], fnb.at[ki], xdev, 9)

    def product_lent(c, k):
        for kk in (k,) if k in (0, 4) else (k, -k):
            ki = ORDER.index(kk)
            if ki not in waited:
                waited.add(ki)
                arrive(("fx", ki), fnb.at[ki])
            part = jnp.dot(fnb[ki], wg[c, blk(0, kk), 0:HALF], preferred_element_type=F32)
            if kk == 0:
                accn[c] = part
            else:
                accn[c] += part
        if k == 4:
            ps[c] = accn[c].astype(BF16)
            send(("pn", c), ps.at[c], pr.at[c], xdev, 9)

    waited = set()

    def loads_once(name):
        if name not in waited:
            waited.add(name)
            loads[name].wait()

    factor_cache = []

    def factor_row():
        if not factor_cache:
            total = jnp.zeros((1, 1), F32)
            for j in range(16):
                digits = wg[0, j, BLK : BLK + 16].astype(F32)
                total = total + (16 * digits[0:1, 0:1] + digits[0:1, 128:129])
            factor_cache.append(jnp.where(live, LOSS_GAIN / (tok_count * total), 0.0))
        return factor_cache[0]

    def scaled(c):
        loads_once("targs")
        arrive(("pn", c), pr.at[c])
        err = acc[c] + pr[c].astype(F32) - targs[:, c * COLS : (c + 1) * COLS].astype(F32)
        st[c] = (err.T * factor_row()).astype(BF16)

    def lend_scaled(c):
        send(("sn", c), st.at[c], stn.at[c], xdev, 9)

    def scatter_span(c, name):
        if name == "b":
            return 0, COLS
        return (0, X_PART[c]) if name == "x" else (X_PART[c], COLS - X_PART[c])

    def share(c, name, k):
        lo, n = scatter_span(c, "x" if name == "c" else name)
        start = blk(name in ("n", "c"), k) * BLK + (0 if name == "b" else HALF)
        cols = pl.ds(pl.multiple_of(start, HALF), HALF)
        val = jnp.dot(st[c, lo : lo + n], feats[:, cols], preferred_element_type=F32)
        if name == "b":
            val = val + jnp.dot(stn[c], fnb[ORDER.index(k)], preferred_element_type=F32)
        return val

    def scatter_cross(c, ki):
        k, n = ORDER[ki], X_PART[c]
        xs[c, ki, 0:n] = share(c, "c", k).astype(BF16)
        send(("rx", c, k), xs.at[c, ki, pl.ds(0, n)], xr.at[c, ki, pl.ds(0, n)], xdev, 4 + c)

    def crossed(c, k, val):
        ki, n = ORDER.index(k), X_PART[c]
        arrive(("rx", c, k), xr.at[c, ki, pl.ds(0, n)])
        return val + xr[c, ki, 0:n].astype(F32)

    def scatter_first(c, name):
        lo, n = scatter_span(c, name)
        col = COLUMN[name]
        if name == "b":
            arrive(("sn", c), stn.at[c])
        val = share(c, name, 4)
        if name == "x":
            val = crossed(c, 4, val)
        z0[c, col, lo : lo + n] = val.astype(BF16)
        group = 6 + c if name == "b" else 4 + c
        for d in (1, -1):
            hlo, hn = part_of(lo, n, d)
            src, dst = z0.at[c, col, pl.ds(hlo, hn)], zr.at[c, lane(d, 1, col), pl.ds(hlo, hn)]
            send(("r", c, d, 1, name), src, dst, zdev[d], group)

    def lane(d, s, col):
        return (16 + (s - 1) * 2 if col == 2 else (s - 1) * 4 + col * 2) + (1 - d) // 2

    def scatter_step(c, s, name, d):
        lo, n = scatter_span(c, name)
        col = COLUMN[name]
        at = lane(d, s, col)
        k = d * (4 - s)
        val = share(c, name, k)
        if name == "x":
            val = crossed(c, k, val)
        if s == 1:
            hlo, hn = part_of(lo, n, d)
            olo, on = part_of(lo, n, -d)
            arrive(("r", c, d, s, name), zr.at[c, at, pl.ds(hlo, hn)])
            zr[c, at, olo : olo + on] = val[olo - lo : olo - lo + on].astype(BF16)
            got = zr[c, at, hlo : hlo + hn].astype(F32)
            zr[c, at, hlo : hlo + hn] = (val[hlo - lo : hlo - lo + hn] + got).astype(BF16)
        else:
            arrive(("r", c, d, s, name), zr.at[c, at, pl.ds(lo, n)])
            zr[c, at, lo : lo + n] = (val + zr[c, at, lo : lo + n].astype(F32)).astype(BF16)
        key = ("r", c, d, s + 1, name) if s < 3 else ("r", c, 4, name)
        send(key, zr.at[c, at, pl.ds(lo, n)], zr.at[c, lane(d, s + 1, col), pl.ds(lo, n)], zdev[d], (6 if col == 2 else 4) + c)

    def scatter_last(c, name):
        lo, n = scatter_span(c, name)
        col = COLUMN[name]
        val = share(c, name, 0)
        if name == "x":
            val = crossed(c, 0, val)
        arrive(("r", c, 4, name), zr.at[c, pl.ds(lane(1, 4, col), 2), pl.ds(lo, n)])
        for d in (1, -1):
            val = val + zr[c, lane(d, 4, col), lo : lo + n].astype(F32)
        if name == "n":
            fxs[c, 0:n] = val.astype(BF16)
            send(("fin", c), fxs.at[c, pl.ds(0, n)], fxr.at[c, pl.ds(0, n)], xdev, 4 + c)
        elif name == "b":
            gt[c, :, 0:HALF] = val
        else:
            gt[c, lo : lo + n, HALF:] = val

    def finish(c):
        lo, n = scatter_span(c, "n")
        if n:
            arrive(("fin", c), fxr.at[c, pl.ds(0, n)])
            gt[c, lo : lo + n, HALF:] += fxr[c, 0:n].astype(F32)
        store(gt.at[c], grad_hbm.at[c])

    stores = []

    def store(src, dst):
        copy = pltpu.make_async_copy(src, dst, store_sem.at[len(stores)])
        copy.start()
        stores.append(copy)

    nb8 = WIDTH // 8 // BLOCK_WIDTH

    def encode():
        loads["exps"].wait()
        loads["pg"].wait()
        signs = sign_table()
        inv = jnp.right_shift(8, exps_ref[...]).astype(F32) * 0.125
        scale = jnp.left_shift(1, exps_ref[...]).astype(F32)
        for p in range(8):
            base = p * nb8
            rows = jnp.concatenate(
                [pg[:, (base + b) * BLOCK_WIDTH : (base + b + 1) * BLOCK_WIDTH] for b in range(nb8)], axis=0
            )
            turned = rotate(rows, signs)
            for b in range(nb8):
                at = slice(b * BLOCK_WIDTH, (b + 1) * BLOCK_WIDTH)
                val = turned[b * 16 : (b + 1) * 16] * inv[:, base + b : base + b + 1]
                enc[p, :, at] = jnp.clip(val, -1.0, 1.0).astype(BF16)
                scl[p, :, at] = jnp.broadcast_to(scale[:, base + b : base + b + 1], (16, BLOCK_WIDTH))
        for k in range(1, 8):
            p = lax.rem(g + k, 8)
            send("enc", enc.at[p], landed.at[k - 1], (xh * 8 + p, f), 8)

    def partial_sum():
        arrive("enc", landed.at[pl.ds(0, 7)])
        total = enc[g].astype(F32)
        for k in range(1, 8):
            total = total + landed[k - 1].astype(F32)
        par_s[...] = total.astype(BF16)
        send("par", par_s, landed.at[7], ((1 - xh) * 8 + g, f), 8)

    def decode():
        arrive("par", landed.at[7])
        val = (par_s[...].astype(F32) + landed[7].astype(F32)) * (1.0 / REPLICAS) * scl[g]
        rows = jnp.concatenate([val[:, b * BLOCK_WIDTH : (b + 1) * BLOCK_WIDTH] for b in range(nb8)], axis=0)
        turned = rotate(rows, sign_table()).astype(BF16)
        mine = pl.ds(pl.multiple_of(g * 1024, 1024), 1024)
        dlt[:, mine] = jnp.concatenate([turned[b * 16 : (b + 1) * 16] for b in range(nb8)], axis=1)
        for k in range(1, 8):
            send("dlt", dlt.at[:, mine], dlt.at[:, mine], (xh * 8 + lax.rem(g + k, 8), f), 8)

    def update():
        arrive("dlt", landed.at[pl.ds(0, 7)])
        store(dlt, delta_hbm)

    steps = {
        "gs": gather_start,
        "gc": gather_cross,
        "gf": gather_forward,
        "gp": product,
        "fx": lend,
        "gq": product_lent,
        "ss": lend_scaled,
        "sc": scaled,
        "rc": scatter_cross,
        "rf": scatter_first,
        "rs": scatter_step,
        "rl": scatter_last,
        "fin": finish,
        "enc": encode,
        "par": partial_sum,
        "dec": decode,
        "upd": update,
    }
    for step in PLAN:
        steps[step[0]](*step[1:])
    assert len(slots) == N_SLOTS, len(slots)

    for c in range(CHUNKS):
        lo, n = gather_span(c, "o")
        sent(c, wg.at[c, pl.ds(0, 15), pl.ds(lo, n)])
        sent(2 + c, wg.at[c, pl.ds(0, 7), pl.ds(0, HALF)])
        sent(4 + c, zr.at[c, pl.ds(0, 15)])
        sent(6 + c, zr.at[c, pl.ds(0, 7)])
    sent(8, landed)
    sent(9, zr.at[0, pl.ds(0, 24)])
    for copy in stores:
        copy.wait()


def finish_kernel(gt_hbm, delta_hbm, params_hbm, moment_hbm, grad_hbm, newp_hbm, newm_hbm, gt, dlt, params, moment, out, newp, newm, load_sem, store_sem):
    loads = [
        pltpu.make_async_copy(gt_hbm.at[c], gt.at[c], load_sem.at[c]) for c in range(CHUNKS)
    ] + [
        pltpu.make_async_copy(delta_hbm, dlt, load_sem.at[CHUNKS]),
        pltpu.make_async_copy(params_hbm, params, load_sem.at[CHUNKS + 1]),
        pltpu.make_async_copy(moment_hbm, moment, load_sem.at[CHUNKS + 2]),
    ]
    for copy in loads:
        copy.start()
    stores = []

    def store(src, dst):
        copy = pltpu.make_async_copy(src, dst, store_sem.at[len(stores)])
        copy.start()
        stores.append(copy)

    for c in range(CHUNKS):
        loads[c].wait()
        out[:, c * COLS : (c + 1) * COLS] = gt[c].T
    store(out, grad_hbm.at[0])
    for copy in loads[CHUNKS:]:
        copy.wait()
    delta = dlt[...].astype(F32)
    new = MOMENTUM * moment[...] + delta
    newm[...] = new
    store(newm, newm_hbm)
    newp[...] = params[...] - OUTER_RATE * (delta + MOMENTUM * new)
    store(newp, newp_hbm)
    for copy in stores:
        copy.wait()


def on_device(features, targets, value_weight, segment_ids, traj_counts, pseudo_grad, block_exps, outer_params, outer_moment):
    hbm = pl.BlockSpec(memory_space=pl.ANY)
    xmax = max(X_PART)
    zmax = COLS - min(X_PART)
    out = pl.pallas_call(
        kernel,
        out_shape=(
            jax.ShapeDtypeStruct((CHUNKS, COLS, BLK), F32),
            jax.ShapeDtypeStruct((16, WIDTH), BF16),
        ),
        in_specs=[hbm] * 7,
        out_specs=(hbm, hbm),
        scratch_shapes=[
            pltpu.VMEM((TOK, WIDTH), BF16),
            pltpu.VMEM((TOK, 2 * COLS), BF16),
            pltpu.VMEM((CHUNKS, 16, BLK + EXTRA, COLS), BF16),
            pltpu.VMEM((CHUNKS, TOK, COLS), F32),
            pltpu.VMEM((CHUNKS, COLS, TOK), BF16),
            pltpu.VMEM((8, TOK, HALF), BF16),
            pltpu.VMEM((CHUNKS, TOK, COLS), F32),
            pltpu.VMEM((CHUNKS, TOK, COLS), BF16),
            pltpu.VMEM((CHUNKS, TOK, COLS), BF16),
            pltpu.VMEM((CHUNKS, COLS, TOK), BF16),
            pltpu.VMEM((CHUNKS, 8, xmax, HALF), BF16),
            pltpu.VMEM((CHUNKS, 8, xmax, HALF), BF16),
            pltpu.VMEM((CHUNKS, 3, COLS, HALF), BF16),
            pltpu.VMEM((CHUNKS, 24, COLS, HALF), BF16),
            pltpu.VMEM((CHUNKS, zmax, HALF), BF16),
            pltpu.VMEM((CHUNKS, zmax, HALF), BF16),
            pltpu.VMEM((CHUNKS, COLS, BLK), F32),
            pltpu.VMEM((CHUNKS, BLK, COLS), F32),
            pltpu.VMEM((16, WIDTH), F32),
            pltpu.VMEM((8, 16, 1024), F32),
            pltpu.VMEM((8, 16, 1024), BF16),
            pltpu.VMEM((15, 16, 1024), BF16),
            pltpu.VMEM((16, 1024), BF16),
            pltpu.VMEM((16, WIDTH), BF16),
            pltpu.VMEM((1, TOK), jnp.int32),
            pltpu.VMEM((1, 8), jnp.int32),
            pltpu.VMEM((16, WIDTH // BLOCK_WIDTH), jnp.int32),
            pltpu.SemaphoreType.DMA((CHUNKS + 6,)),
            pltpu.SemaphoreType.DMA((3,)),
            pltpu.SemaphoreType.DMA((10,)),
            pltpu.SemaphoreType.DMA((N_SLOTS,)),
        ],
        compiler_params=pltpu.CompilerParams(
            collective_id=0, has_side_effects=True, vmem_limit_bytes=56 * 2**20
        ),
    )(features, targets, value_weight, segment_ids, traj_counts, pseudo_grad, block_exps)
    wide = pltpu.VMEM((16, WIDTH), F32)
    return pl.pallas_call(
        finish_kernel,
        out_shape=(
            jax.ShapeDtypeStruct((1, BLK, CHUNKS * COLS), F32),
            jax.ShapeDtypeStruct((16, WIDTH), F32),
            jax.ShapeDtypeStruct((16, WIDTH), F32),
        ),
        in_specs=[hbm] * 4,
        out_specs=(hbm,) * 3,
        scratch_shapes=[
            pltpu.VMEM((CHUNKS, COLS, BLK), F32),
            pltpu.VMEM((16, WIDTH), BF16),
            wide,
            wide,
            pltpu.VMEM((BLK, CHUNKS * COLS), F32),
            wide,
            wide,
            pltpu.SemaphoreType.DMA((CHUNKS + 3,)),
            pltpu.SemaphoreType.DMA((3,)),
        ],
        compiler_params=pltpu.CompilerParams(vmem_limit_bytes=60 * 2**20),
    )(*out, outer_params, outer_moment)


def solution(mesh):
    return jax.shard_map(
        on_device,
        mesh=mesh,
        in_specs=(
            P("rep", "fsdp", None),
            P("rep", "fsdp", None),
            P("rep", "fsdp", None),
            P("rep", "fsdp"),
            P("rep", "fsdp"),
            P("rep", "fsdp", None),
            P("fsdp", None),
            P("fsdp", None),
            P("fsdp", None),
        ),
        out_specs=(P("rep", "fsdp", None), P("fsdp", None), P("fsdp", None)),
        check_vma=False,
    )
```
